1024 devices in a mesh: dp: 64 (over z, x), tensor: 16 (over y, core).
Axes of the slice: x: 8, y: 8, z: 8, core: 2. Of those that a mesh axis runs over, the one named last changes fastest.
Arguments:
- grads: bfloat16 [64, 1024, 8192], P('dp', None, 'tensor'), may hold values from -60 to 60
- errors: bfloat16 [64, 1024, 8192], P('dp', None, 'tensor'), may hold values from -3 to 3
- q_in: float32 [1024, 4], replicated, may hold values from -6 to 6
Outputs:
- new_error: bfloat16 [64, 1024, 8192], P('dp', None, 'tensor')
- right_factor: float32 [8192, 4], P('tensor')
- new_q: float32 [1024, 4], replicated
The draws below stay inside these ranges and needn't reach their ends.
All inputs are finite; a program needn't handle non-finite values.
Results may differ from the reference program's by a relative error of at most 0.001.
Values sent between devices are 32-bit elements; how exact they have to be, the bound alone decides.
No kernel may reach another device: no remote copies, remote signals or barrier semaphores. Data moves between devices by JAX's collectives and lax.ppermute only.
A program may use at most 32 MiB of HBM per device.

```python
import math
import jax
import jax.numpy as jnp
from jax import lax

ROWS = 1024
COLS = 8192
RANK = 4
REPLICAS = 64


def draw_grads(key, part):
    key = jax.random.fold_in(key, 11)
    key_rows, key_cols, key_noise = jax.random.split(key, 3)
    row_scale = jnp.exp(jax.random.uniform(key_rows, (1, ROWS, 1), jnp.float32, 0.0, 1.2))
    ramp = 1.0 + 2.0 * jnp.arange(COLS, dtype=jnp.float32) / COLS
    col_scale = jnp.exp(jax.random.uniform(key_cols, (1, 1, COLS), jnp.float32, 0.0, 1.2)) * ramp[None, None, :]
    replica_scale = (1.0 + 2.0 * jnp.arange(REPLICAS, dtype=jnp.float32) / REPLICAS)[:, None, None]
    noise = jax.random.normal(key_noise, (REPLICAS, ROWS, COLS), jnp.float32)
    values = 0.1 * noise * row_scale * col_scale * replica_scale
    return jnp.clip(values, -60.0, 60.0).astype(jnp.bfloat16)


def block_scale(key, extent, shards, low, top_value):
    def one(dim, parts):
        draws = jax.random.uniform(jax.random.fold_in(jax.random.fold_in(key, 6), dim), (parts,), jnp.float32, low / len(shards), top_value / len(shards))
        return jnp.repeat(jnp.exp(draws), extent[dim] // parts).reshape((-1,) + (1,) * (len(extent) - dim - 1))

    loudness = one(*shards[0])
    for cut in shards[1:]:
        loudness = loudness * one(*cut)
    return loudness


def scatter_about(rng, dims, width, limit, shards=(), kind=jnp.bfloat16):
    array = width * jax.random.normal(rng, dims, jnp.float32)
    if shards:
        array = array * block_scale(rng, dims, shards, -0.22, 0.18)
    return jnp.clip(array, -limit, limit).astype(kind)


def setup_inputs(seed: int = 0) -> dict:
    key_of = jax.random.split(jax.random.key(seed), 4)
    grads = draw_grads(jax.random.fold_in(key_of[3], 71), 0)
    errors = scatter_about(key_of[1], (REPLICAS, ROWS, COLS), 0.5, 3.0, ((0, 64), (2, 16)))
    q_in = scatter_about(key_of[2], (ROWS, RANK), 1.0, 6.0, (), jnp.float32)
    return dict(grads=grads, errors=errors, q_in=q_in)


def reference(grads, errors, q_in):
    merged = grads.astype(jnp.float32) + errors.astype(jnp.float32)
    left = jnp.einsum('inm,nr->mr', merged, q_in, precision=lax.Precision.HIGHEST) / REPLICAS
    gram = jnp.dot(left.T, left, precision=lax.Precision.HIGHEST)
    lower = jnp.linalg.cholesky(gram)
    identity_matrix = jnp.eye(RANK, dtype=jnp.float32)
    inverse = jax.scipy.linalg.solve_triangular(lower, identity_matrix, lower=True)
    right = jnp.dot(left, inverse.T, precision=lax.Precision.HIGHEST)
    new_q = jnp.einsum('inm,mr->nr', merged, right, precision=lax.Precision.HIGHEST) / REPLICAS
    approx = jnp.dot(new_q, right.T, precision=lax.Precision.HIGHEST)
    new_error = (merged - approx[None]).astype(jnp.bfloat16)
    return (new_error, right * math.sqrt(COLS), new_q)
```

```python
import math

import jax
import jax.numpy as jnp
from jax import lax
from jax.sharding import Mesh
from jax.sharding import PartitionSpec as P

COLS = 8192
RANK = 4
LANES = 128


def sum_over(value, axis):
    peers = lax.axis_size(axis)
    copies = jnp.broadcast_to(value[None], (peers,) + value.shape)
    return jnp.sum(lax.all_to_all(copies, axis, 0, 0, tiled=True), axis=0)


def on_device(grads, errors, q_in):
    replicas = lax.axis_size("z") * lax.axis_size("x")
    matrix = grads[0].astype(jnp.float32) + errors[0].astype(jnp.float32)
    rows, cols = matrix.shape
    local_left = lax.dot_general(
        q_in, matrix, (((0,), (0,)), ((), ())), precision=lax.Precision.HIGHEST, preferred_element_type=jnp.float32
    )
    left = local_left.reshape(-1, LANES)
    for axis in ("x", "z"):
        left = sum_over(left, axis)
    left = left.reshape(RANK, cols) / replicas

    local_gram = jnp.dot(left, left.T, precision=lax.Precision.HIGHEST)
    local_back = lax.dot_general(
        left, matrix, (((1,), (1,)), ((), ())), precision=lax.Precision.HIGHEST, preferred_element_type=jnp.float32
    )
    terms = jnp.concatenate([local_back.reshape(-1), local_gram.reshape(-1)])
    terms = jnp.pad(terms, (0, -terms.size % (8 * LANES))).reshape(-1, LANES)
    terms = jnp.sum(lax.all_gather(terms, "core"), axis=0)
    terms = sum_over(terms, "y")
    back_rows = rows * RANK // LANES
    gram = terms[back_rows, : RANK * RANK].reshape(RANK, RANK)
    back = terms[:back_rows]
    for axis in ("x", "z"):
        back = sum_over(back, axis)

    lower = jnp.linalg.cholesky(gram)
    inverse = jax.scipy.linalg.solve_triangular(lower, jnp.eye(RANK, dtype=jnp.float32), lower=True)
    right = jnp.dot(inverse, left, precision=lax.Precision.HIGHEST)
    new_q = jnp.dot(inverse, back.reshape(RANK, rows), precision=lax.Precision.HIGHEST) / replicas
    approx = lax.dot_general(
        new_q, right, (((0,), (0,)), ((), ())), precision=lax.Precision.HIGHEST, preferred_element_type=jnp.float32
    )
    new_error = (matrix - approx).astype(jnp.bfloat16)[None]
    return (new_error, (right * math.sqrt(COLS)).T, new_q.T)


def solution(mesh):
    physical = Mesh(mesh.devices.reshape(8, 8, 8, 2), ("z", "x", "y", "core"))
    dp, tensor = ("z", "x"), ("y", "core")
    return jax.shard_map(
        on_device,
        mesh=physical,
        in_specs=(P(dp, None, tensor), P(dp, None, tensor), P()),
        out_specs=(P(dp, None, tensor), P(tensor, None), P()),
        check_vma=False,
    )
```

```python
import functools
import math

import jax
import jax.numpy as jnp
from jax import lax
from jax.experimental import pallas as pl
from jax.experimental.pallas import tpu as pltpu
from jax.sharding import Mesh
from jax.sharding import PartitionSpec as P

COLS = 8192
RANK = 4
LANES = 128
CHUNKS = 4
VMEM = pl.BlockSpec(memory_space=pltpu.VMEM)
HBM = pl.BlockSpec(memory_space=pltpu.HBM)


def pieces_of(value):
    high = value.astype(jnp.bfloat16).astype(jnp.float32)
    rest = value - high
    middle = rest.astype(jnp.bfloat16).astype(jnp.float32)
    low = (rest - middle).astype(jnp.bfloat16).astype(jnp.float32)
    return high, middle, low


def stacked(*rows):
    rows += (jnp.zeros_like(rows[0]),) * (-len(rows) % (16 // RANK))
    return jnp.concatenate(rows, axis=0).astype(jnp.bfloat16)


def unstacked_sum(products):
    return products[:RANK] + (products[RANK : 2 * RANK] + products[2 * RANK : 3 * RANK])


def to_blocks(ref, value):
    for block in range(value.shape[1] // LANES):
        ref[block * RANK : (block + 1) * RANK, :] = value[:, block * LANES : (block + 1) * LANES]


def from_blocks(value):
    blocks = [value[row : row + RANK] for row in range(0, value.shape[0], RANK)]
    return jnp.concatenate(blocks, axis=1)


def left_kernel(q_hbm, grads_hbm, errors_hbm, left_ref, grads_ref, errors_ref, q_ref, q_sem, sems):
    rows, cols = grads_ref.shape
    step = rows // CHUNKS
    q_copy = pltpu.make_async_copy(q_hbm, q_ref, q_sem)
    q_copy.start()
    copies = []
    for chunk in range(CHUNKS):
        part = pl.ds(chunk * step, step)
        for which, (source, target) in enumerate(((grads_hbm, grads_ref), (errors_hbm, errors_ref))):
            copy = pltpu.make_async_copy(source.at[0, part, :], target.at[part, :], sems.at[chunk, which])
            copy.start()
            copies.append(copy)
    q_copy.wait()
    q = stacked(*pieces_of(q_ref[...]))
    total = jnp.zeros((q.shape[0], cols), jnp.float32)
    for chunk in range(CHUNKS):
        part = pl.ds(chunk * step, step)
        for which, source in enumerate((grads_ref, errors_ref)):
            copies[2 * chunk + which].wait()
            total += jnp.dot(
                q[:, chunk * step : (chunk + 1) * step], source[part, :], preferred_element_type=jnp.float32
            )
    to_blocks(left_ref, unstacked_sum(total))


def back_kernel(replicas, parts_ref, grads_ref, errors_ref, left_ref, terms_ref):
    left = from_blocks(jnp.sum(parts_ref[...], axis=0)) * (1.0 / replicas)
    left_ref[...] = left
    stack = stacked(*pieces_of(left))
    across = (((1,), (1,)), ((), ()))
    total = lax.dot_general(stack, grads_ref[...], across, preferred_element_type=jnp.float32)
    total += lax.dot_general(stack, errors_ref[...], across, preferred_element_type=jnp.float32)
    back = unstacked_sum(total)
    gram = lax.dot_general(
        left, left, across, precision=lax.Precision.HIGHEST, preferred_element_type=jnp.float32
    )
    used = back.shape[1] // LANES * RANK
    to_blocks(terms_ref, back)
    terms_ref[used:, :] = jnp.zeros((terms_ref.shape[0] - used, LANES), jnp.float32)
    terms_ref[used : used + RANK, :RANK] = gram


def error_kernel(
    replicas, parts_ref, gram_ref, left_ref, grads_ref, errors_ref, out_hbm, right_ref, q_ref, out_ref, sems
):
    rows, cols = grads_ref.shape
    back = from_blocks(jnp.sum(parts_ref[...], axis=0))
    work = jnp.concatenate([gram_ref[:RANK, :], left_ref[...], back], axis=1)
    row = lax.broadcasted_iota(jnp.int32, (RANK, 1), 0)
    for k in range(RANK):
        scale = 1.0 / jnp.sqrt(work[k : k + 1, k : k + 1])
        column = jnp.where(row > k, work[:, k : k + 1] * scale, 0.0)
        solved = work[k : k + 1, :] * scale
        work = jnp.where(row == k, solved, work - column * solved)
    right = work[:, LANES : LANES + cols]
    new_q = work[:, LANES + cols :] * (1.0 / replicas)
    right_ref[...] = right * math.sqrt(COLS)
    q_ref[...] = new_q
    q1, q2, q3 = pieces_of(new_q)
    r1, r2, r3 = pieces_of(right)
    tall = stacked(q1, q1, q2, q2, q1, q3)
    wide = stacked(r1, r2, r1, r2, r3, r1)
    step = rows // CHUNKS
    copies = []
    for chunk in range(CHUNKS):
        part = pl.ds(chunk * step, step)
        approx = lax.dot_general(
            tall[:, chunk * step : (chunk + 1) * step],
            wide,
            (((0,), (0,)), ((), ())),
            preferred_element_type=jnp.float32,
        )
        merged = grads_ref[part, :].astype(jnp.float32) + errors_ref[part, :].astype(jnp.float32)
        out_ref[part, :] = (merged - approx).astype(jnp.bfloat16)
        copy = pltpu.make_async_copy(out_ref.at[part, :], out_hbm.at[0, part, :], sems.at[chunk])
        copy.start()
        copies.append(copy)
    for copy in copies:
        copy.wait()


def copies_for(value, axis):
    return jnp.broadcast_to(value[None], (lax.axis_size(axis),) + value.shape)


def exchange(value, axis):
    return lax.all_to_all(copies_for(value, axis), axis, 0, 0, tiled=True)


def on_device(grads, errors, q_in):
    replicas = lax.axis_size("z") * lax.axis_size("x")
    _, rows, cols = grads.shape
    f32, bf16 = jnp.float32, jnp.bfloat16
    left_rows, back_rows = RANK * cols // LANES, RANK * rows // LANES
    limit = pltpu.CompilerParams(vmem_limit_bytes=32 * 2**20)

    left, grads_near, errors_near = pl.pallas_call(
        left_kernel,
        out_shape=(
            pltpu.VMEM((left_rows, LANES), f32),
            pltpu.VMEM((rows, cols), bf16),
            pltpu.VMEM((rows, cols), bf16),
        ),
        in_specs=[HBM] * 3,
        out_specs=(VMEM, VMEM, VMEM),
        scratch_shapes=[pltpu.VMEM((RANK, rows), f32), pltpu.SemaphoreType.DMA, pltpu.SemaphoreType.DMA((CHUNKS, 2))],
        compiler_params=limit,
        name="left",
    )(*(pltpu.with_memory_space_constraint(x, pltpu.HBM) for x in (q_in.T, grads, errors)))

    left = jnp.sum(exchange(left, "x"), axis=0)
    left, terms = pl.pallas_call(
        functools.partial(back_kernel, replicas),
        out_shape=(pltpu.VMEM((RANK, cols), f32), pltpu.VMEM((back_rows + 8, LANES), f32)),
        in_specs=[VMEM] * 3,
        out_specs=(VMEM, VMEM),
        compiler_params=limit,
        name="back",
    )(exchange(left, "z"), grads_near, errors_near)

    terms = jnp.sum(lax.all_gather(terms, "core"), axis=0)
    terms = jnp.sum(exchange(terms, "y"), axis=0)
    gram, back = terms[back_rows:], terms[:back_rows]
    back = jnp.sum(exchange(back, "x"), axis=0)

    new_error, right_factor, new_q = pl.pallas_call(
        functools.partial(error_kernel, replicas),
        out_shape=(
            jax.ShapeDtypeStruct((1, rows, cols), bf16),
            jax.ShapeDtypeStruct((RANK, cols), f32),
            jax.ShapeDtypeStruct((RANK, rows), f32),
        ),
        in_specs=[VMEM] * 5,
        out_specs=(HBM, VMEM, VMEM),
        scratch_shapes=[pltpu.VMEM((rows, cols), bf16), pltpu.SemaphoreType.DMA((CHUNKS,))],
        compiler_params=limit,
        name="error",
    )(exchange(back, "z"), gram, left, grads_near, errors_near)
    return new_error, right_factor.T, new_q.T


def solution(mesh):
    physical = Mesh(mesh.devices.reshape(8, 8, 8, 2), ("z", "x", "y", "core"))
    dp, tensor = ("z", "x"), ("y", "core")
    return jax.shard_map(
        on_device,
        mesh=physical,
        in_specs=(P(dp, None, tensor), P(dp, None, tensor), P()),
        out_specs=(P(dp, None, tensor), P(tensor, None), P()),
        check_vma=False,
    )
```

```python
import functools
import math

import jax
import jax.numpy as jnp
from jax import lax
from jax.experimental import pallas as pl
from jax.experimental.pallas import tpu as pltpu
from jax.sharding import Mesh
from jax.sharding import PartitionSpec as P

COLS = 8192
RANK = 4
LANES = 128
CHUNKS = 4
SENDER = 1
VMEM = pl.BlockSpec(memory_space=pltpu.VMEM)
HBM = pl.BlockSpec(memory_space=pltpu.HBM)


def pieces_of(value):
    high = value.astype(jnp.bfloat16).astype(jnp.float32)
    rest = value - high
    middle = rest.astype(jnp.bfloat16).astype(jnp.float32)
    low = (rest - middle).astype(jnp.bfloat16).astype(jnp.float32)
    return high, middle, low


def stacked(*rows):
    rows += (jnp.zeros_like(rows[0]),) * (-len(rows) % (16 // RANK))
    return jnp.concatenate(rows, axis=0).astype(jnp.bfloat16)


def unstacked_sum(products):
    return products[:RANK] + (products[RANK : 2 * RANK] + products[2 * RANK : 3 * RANK])


def to_blocks(ref, value):
    for block in range(value.shape[1] // LANES):
        ref[block * RANK : (block + 1) * RANK, :] = value[:, block * LANES : (block + 1) * LANES]


def from_blocks(value):
    blocks = [value[row : row + RANK] for row in range(0, value.shape[0], RANK)]
    return jnp.concatenate(blocks, axis=1)


def left_kernel(q_hbm, grads_hbm, errors_hbm, left_ref, grads_ref, errors_ref, q_ref, q_sem, sems):
    rows, cols = grads_ref.shape
    step = rows // CHUNKS
    q_copy = pltpu.make_async_copy(q_hbm, q_ref, q_sem)
    q_copy.start()
    copies = []
    for chunk in range(CHUNKS):
        part = pl.ds(chunk * step, step)
        for which, (source, target) in enumerate(((grads_hbm, grads_ref), (errors_hbm, errors_ref))):
            copy = pltpu.make_async_copy(source.at[0, part, :], target.at[part, :], sems.at[chunk, which])
            copy.start()
            copies.append(copy)
    q_copy.wait()
    q = stacked(*pieces_of(q_ref[...]))
    total = jnp.zeros((q.shape[0], cols), jnp.float32)
    for chunk in range(CHUNKS):
        part = pl.ds(chunk * step, step)
        for which, source in enumerate((grads_ref, errors_ref)):
            copies[2 * chunk + which].wait()
            total += jnp.dot(
                q[:, chunk * step : (chunk + 1) * step], source[part, :], preferred_element_type=jnp.float32
            )
    to_blocks(left_ref, unstacked_sum(total))


def back_kernel(replicas, parts_ref, grads_ref, errors_ref, left_ref, terms_ref):
    left = from_blocks(jnp.sum(parts_ref[...], axis=0)) * (1.0 / replicas)
    left_ref[...] = left
    stack = stacked(*pieces_of(left))
    across = (((1,), (1,)), ((), ()))
    total = lax.dot_general(stack, grads_ref[...], across, preferred_element_type=jnp.float32)
    total += lax.dot_general(stack, errors_ref[...], across, preferred_element_type=jnp.float32)
    back = unstacked_sum(total)
    gram = lax.dot_general(
        left, left, across, precision=lax.Precision.HIGHEST, preferred_element_type=jnp.float32
    )
    used = back.shape[1] // LANES * RANK
    to_blocks(terms_ref, back)
    terms_ref[used:, :] = jnp.zeros((terms_ref.shape[0] - used, LANES), jnp.float32)
    terms_ref[used : used + RANK, :RANK] = gram


def error_kernel(
    replicas, terms_ref, left_ref, grads_ref, errors_ref, out_hbm, right_ref, q_ref, out_ref, sems
):
    rows, cols = grads_ref.shape
    used = rows // LANES * RANK
    back = from_blocks(terms_ref[SENDER, :used, :])
    gram = terms_ref[SENDER, used : used + RANK, :]
    work = jnp.concatenate([gram, left_ref[...], back], axis=1)
    row = lax.broadcasted_iota(jnp.int32, (RANK, 1), 0)
    for k in range(RANK):
        scale = 1.0 / jnp.sqrt(work[k : k + 1, k : k + 1])
        column = jnp.where(row > k, work[:, k : k + 1] * scale, 0.0)
        solved = work[k : k + 1, :] * scale
        work = jnp.where(row == k, solved, work - column * solved)
    right = work[:, LANES : LANES + cols]
    new_q = work[:, LANES + cols :] * (1.0 / replicas)
    right_ref[...] = right * math.sqrt(COLS)
    q_ref[...] = new_q
    q1, q2, q3 = pieces_of(new_q)
    r1, r2, r3 = pieces_of(right)
    tall = stacked(q1, q1, q2, q2, q1, q3)
    wide = stacked(r1, r2, r1, r2, r3, r1)
    step = rows // CHUNKS
    copies = []
    for chunk in range(CHUNKS):
        part = pl.ds(chunk * step, step)
        approx = lax.dot_general(
            tall[:, chunk * step : (chunk + 1) * step],
            wide,
            (((0,), (0,)), ((), ())),
            preferred_element_type=jnp.float32,
        )
        merged = grads_ref[part, :].astype(jnp.float32) + errors_ref[part, :].astype(jnp.float32)
        out_ref[part, :] = (merged - approx).astype(jnp.bfloat16)
        copy = pltpu.make_async_copy(out_ref.at[part, :], out_hbm.at[0, part, :], sems.at[chunk])
        copy.start()
        copies.append(copy)
    for copy in copies:
        copy.wait()


def copies_for(value, axis):
    return jnp.broadcast_to(value[None], (lax.axis_size(axis),) + value.shape)


def exchange(value, axis):
    return lax.all_to_all(copies_for(value, axis), axis, 0, 0, tiled=True)


def on_device(grads, errors, q_in):
    replicas = lax.axis_size("z") * lax.axis_size("x")
    _, rows, cols = grads.shape
    f32, bf16 = jnp.float32, jnp.bfloat16
    left_rows, back_rows = RANK * cols // LANES, RANK * rows // LANES
    limit = pltpu.CompilerParams(vmem_limit_bytes=32 * 2**20)

    left, grads_near, errors_near = pl.pallas_call(
        left_kernel,
        out_shape=(
            pltpu.VMEM((left_rows, LANES), f32),
            pltpu.VMEM((rows, cols), bf16),
            pltpu.VMEM((rows, cols), bf16),
        ),
        in_specs=[HBM] * 3,
        out_specs=(VMEM, VMEM, VMEM),
        scratch_shapes=[pltpu.VMEM((RANK, rows), f32), pltpu.SemaphoreType.DMA, pltpu.SemaphoreType.DMA((CHUNKS, 2))],
        compiler_params=limit,
        name="left",
    )(*(pltpu.with_memory_space_constraint(x, pltpu.HBM) for x in (q_in.T, grads, errors)))

    left = jnp.sum(exchange(left, "x"), axis=0)
    left, terms = pl.pallas_call(
        functools.partial(back_kernel, replicas),
        out_shape=(pltpu.VMEM((RANK, cols), f32), pltpu.VMEM((back_rows + 8, LANES), f32)),
        in_specs=[VMEM] * 3,
        out_specs=(VMEM, VMEM),
        compiler_params=limit,
        name="back",
    )(exchange(left, "z"), grads_near, errors_near)

    terms = jnp.sum(lax.all_gather(terms, "core"), axis=0)

    def over_chips(terms):
        terms = jnp.sum(exchange(terms, "y"), axis=0)
        back = jnp.sum(exchange(terms[:back_rows], "x"), axis=0)
        back = jnp.sum(exchange(back, "z"), axis=0)
        return jnp.concatenate([back, terms[back_rows:]])

    terms = lax.cond(lax.axis_index("core") == SENDER, over_chips, lambda terms: terms, terms)
    terms = lax.all_gather(terms, "core")

    new_error, right_factor, new_q = pl.pallas_call(
        functools.partial(error_kernel, replicas),
        out_shape=(
            jax.ShapeDtypeStruct((1, rows, cols), bf16),
            jax.ShapeDtypeStruct((RANK, cols), f32),
            jax.ShapeDtypeStruct((RANK, rows), f32),
        ),
        in_specs=[VMEM] * 4,
        out_specs=(HBM, VMEM, VMEM),
        scratch_shapes=[pltpu.VMEM((rows, cols), bf16), pltpu.SemaphoreType.DMA((CHUNKS,))],
        compiler_params=limit,
        name="error",
    )(terms, left, grads_near, errors_near)
    return new_error, right_factor.T, new_q.T


def solution(mesh):
    physical = Mesh(mesh.devices.reshape(8, 8, 8, 2), ("z", "x", "y", "core"))
    dp, tensor = ("z", "x"), ("y", "core")
    return jax.shard_map(
        on_device,
        mesh=physical,
        in_specs=(P(dp, None, tensor), P(dp, None, tensor), P()),
        out_specs=(P(dp, None, tensor), P(tensor, None), P()),
        check_vma=False,
    )
```

```python
import functools
import math

import jax
import jax.numpy as jnp
from jax import lax
from jax.experimental import pallas as pl
from jax.experimental.pallas import tpu as pltpu
from jax.sharding import Mesh
from jax.sharding import PartitionSpec as P

COLS = 8192
RANK = 4
LANES = 128
CHUNKS = 4
SENDER = 1
VMEM = pl.BlockSpec(memory_space=pltpu.VMEM)
HBM = pl.BlockSpec(memory_space=pltpu.HBM)


def pieces_of(value):
    high = value.astype(jnp.bfloat16).astype(jnp.float32)
    rest = value - high
    middle = rest.astype(jnp.bfloat16).astype(jnp.float32)
    low = (rest - middle).astype(jnp.bfloat16).astype(jnp.float32)
    return high, middle, low


def stacked(*rows):
    rows += (jnp.zeros_like(rows[0]),) * (-len(rows) % (16 // RANK))
    return jnp.concatenate(rows, axis=0).astype(jnp.bfloat16)


def unstacked_sum(products):
    return products[:RANK] + (products[RANK : 2 * RANK] + products[2 * RANK : 3 * RANK])


def to_blocks(ref, value):
    for block in range(value.shape[1] // LANES):
        ref[block * RANK : (block + 1) * RANK, :] = value[:, block * LANES : (block + 1) * LANES]


def from_blocks(value):
    blocks = [value[row : row + RANK] for row in range(0, value.shape[0], RANK)]
    return jnp.concatenate(blocks, axis=1)


def left_kernel(q_hbm, grads_hbm, errors_hbm, left_ref, grads_ref, errors_ref, q_ref, q_sem, sems):
    rows, cols = grads_ref.shape
    step = rows // CHUNKS
    q_copy = pltpu.make_async_copy(q_hbm, q_ref, q_sem)
    q_copy.start()
    copies = []
    for chunk in range(CHUNKS):
        part = pl.ds(chunk * step, step)
        for which, (source, target) in enumerate(((grads_hbm, grads_ref), (errors_hbm, errors_ref))):
            copy = pltpu.make_async_copy(source.at[0, part, :], target.at[part, :], sems.at[chunk, which])
            copy.start()
            copies.append(copy)
    q_copy.wait()
    q = stacked(*pieces_of(q_ref[...]))
    total = jnp.zeros((q.shape[0], cols), jnp.float32)
    for chunk in range(CHUNKS):
        part = pl.ds(chunk * step, step)
        for which, source in enumerate((grads_ref, errors_ref)):
            copies[2 * chunk + which].wait()
            total += jnp.dot(
                q[:, chunk * step : (chunk + 1) * step], source[part, :], preferred_element_type=jnp.float32
            )
    to_blocks(left_ref, unstacked_sum(total))


def back_kernel(replicas, parts_ref, grads_ref, errors_ref, left_ref, terms_ref):
    left = from_blocks(jnp.sum(parts_ref[...], axis=0)) * (1.0 / replicas)
    left_ref[...] = left
    stack = stacked(*pieces_of(left))
    across = (((1,), (1,)), ((), ()))
    total = lax.dot_general(stack, grads_ref[...], across, preferred_element_type=jnp.float32)
    total += lax.dot_general(stack, errors_ref[...], across, preferred_element_type=jnp.float32)
    back = unstacked_sum(total)
    gram = lax.dot_general(
        left, left, across, precision=lax.Precision.HIGHEST, preferred_element_type=jnp.float32
    )
    used = back.shape[1] // LANES * RANK
    to_blocks(terms_ref, back)
    terms_ref[used:, :] = jnp.zeros((terms_ref.shape[0] - used, LANES), jnp.float32)
    terms_ref[used : used + RANK, :RANK] = gram


def join_kernel(parts_ref, terms_ref, out_ref):
    used = parts_ref.shape[1]
    out_ref[:used, :] = jnp.sum(parts_ref[...], axis=0)
    out_ref[used:, :] = terms_ref[used:, :]


def error_kernel(
    replicas, terms_ref, left_ref, grads_ref, errors_ref, out_hbm, right_hbm, q_hbm, out_ref, right_ref, q_ref, sems
):
    rows, cols = grads_ref.shape
    used = rows // LANES * RANK
    back = from_blocks(terms_ref[SENDER, :used, :])
    gram = terms_ref[SENDER, used : used + RANK, :]
    work = jnp.concatenate([gram, left_ref[...], back], axis=1)
    row = lax.broadcasted_iota(jnp.int32, (RANK, 1), 0)
    for k in range(RANK):
        scale = 1.0 / jnp.sqrt(work[k : k + 1, k : k + 1])
        column = jnp.where(row > k, work[:, k : k + 1] * scale, 0.0)
        solved = work[k : k + 1, :] * scale
        work = jnp.where(row == k, solved, work - column * solved)
    right = work[:, LANES : LANES + cols]
    new_q = work[:, LANES + cols :] * (1.0 / replicas)
    right_ref[...] = right * math.sqrt(COLS)
    q_ref[...] = new_q
    copies = [
        pltpu.make_async_copy(right_ref, right_hbm, sems.at[CHUNKS]),
        pltpu.make_async_copy(q_ref, q_hbm, sems.at[CHUNKS + 1]),
    ]
    for copy in copies:
        copy.start()
    q1, q2, q3 = pieces_of(new_q)
    r1, r2, r3 = pieces_of(right)
    tall = stacked(q1, q1, q2, q2, q1, q3)
    wide = stacked(r1, r2, r1, r2, r3, r1)
    step = rows // CHUNKS
    for chunk in range(CHUNKS):
        part = pl.ds(chunk * step, step)
        approx = lax.dot_general(
            tall[:, chunk * step : (chunk + 1) * step],
            wide,
            (((0,), (0,)), ((), ())),
            preferred_element_type=jnp.float32,
        )
        merged = grads_ref[part, :].astype(jnp.float32) + errors_ref[part, :].astype(jnp.float32)
        out_ref[part, :] = (merged - approx).astype(jnp.bfloat16)
        copy = pltpu.make_async_copy(out_ref.at[part, :], out_hbm.at[0, part, :], sems.at[chunk])
        copy.start()
        copies.append(copy)
    for copy in copies:
        copy.wait()


def copies_for(value, axis):
    return jnp.broadcast_to(value[None], (lax.axis_size(axis),) + value.shape)


def exchange(value, axis):
    return lax.all_to_all(copies_for(value, axis), axis, 0, 0, tiled=True)


def on_device(grads, errors, q_in):
    replicas = lax.axis_size("z") * lax.axis_size("x")
    _, rows, cols = grads.shape
    f32, bf16 = jnp.float32, jnp.bfloat16
    left_rows, back_rows = RANK * cols // LANES, RANK * rows // LANES
    limit = pltpu.CompilerParams(vmem_limit_bytes=32 * 2**20)
    q_in, core = lax.optimization_barrier((q_in, lax.axis_index("core")))

    left, grads_near, errors_near = pl.pallas_call(
        left_kernel,
        out_shape=(
            pltpu.VMEM((left_rows, LANES), f32),
            pltpu.VMEM((rows, cols), bf16),
            pltpu.VMEM((rows, cols), bf16),
        ),
        in_specs=[HBM] * 3,
        out_specs=(VMEM, VMEM, VMEM),
        scratch_shapes=[pltpu.VMEM((RANK, rows), f32), pltpu.SemaphoreType.DMA, pltpu.SemaphoreType.DMA((CHUNKS, 2))],
        compiler_params=limit,
        name="left",
    )(*(pltpu.with_memory_space_constraint(x, pltpu.HBM) for x in (q_in.T, grads, errors)))

    left = jnp.sum(exchange(left, "x"), axis=0)
    left, terms = pl.pallas_call(
        functools.partial(back_kernel, replicas),
        out_shape=(
            pltpu.VMEM((RANK, cols), f32),
            pltpu.VMEM((back_rows + 8, LANES), f32),
        ),
        in_specs=[VMEM] * 3,
        out_specs=(VMEM, VMEM),
        compiler_params=limit,
        name="back",
    )(exchange(left, "z"), grads_near, errors_near)

    terms = jnp.sum(lax.all_gather(terms, "core"), axis=0)

    def over_chips(terms):
        terms = jnp.sum(exchange(terms, "y"), axis=0)
        back = jnp.sum(exchange(terms[:back_rows], "x"), axis=0)
        return pl.pallas_call(
            join_kernel,
            out_shape=pltpu.VMEM(terms.shape, f32),
            in_specs=[VMEM] * 2,
            out_specs=VMEM,
            compiler_params=limit,
            name="join",
        )(exchange(back, "z"), terms)

    terms, core = lax.optimization_barrier((terms, core))
    terms = lax.cond(core == SENDER, over_chips, lambda terms: terms, terms)
    terms = lax.all_gather(terms, "core")

    new_error, right_factor, new_q = pl.pallas_call(
        functools.partial(error_kernel, replicas),
        out_shape=(
            jax.ShapeDtypeStruct((1, rows, cols), bf16),
            jax.ShapeDtypeStruct((RANK, cols), f32),
            jax.ShapeDtypeStruct((RANK, rows), f32),
        ),
        in_specs=[VMEM] * 4,
        out_specs=(HBM, HBM, HBM),
        scratch_shapes=[
            pltpu.VMEM((rows, cols), bf16),
            pltpu.VMEM((RANK, cols), f32),
            pltpu.VMEM((RANK, rows), f32),
            pltpu.SemaphoreType.DMA((CHUNKS + 2,)),
        ],
        compiler_params=limit,
        name="error",
    )(terms, left, grads_near, errors_near)
    return new_error, right_factor.T, new_q.T


def solution(mesh):
    physical = Mesh(mesh.devices.reshape(8, 8, 8, 2), ("z", "x", "y", "core"))
    dp, tensor = ("z", "x"), ("y", "core")
    return jax.shard_map(
        on_device,
        mesh=physical,
        in_specs=(P(dp, None, tensor), P(dp, None, tensor), P()),
        out_specs=(P(dp, None, tensor), P(tensor, None), P()),
        check_vma=False,
    )
```

```python
import functools
import math

import jax
import jax.numpy as jnp
from jax import lax
from jax.experimental import pallas as pl
from jax.experimental.pallas import tpu as pltpu
from jax.sharding import Mesh
from jax.sharding import PartitionSpec as P

COLS = 8192
RANK = 4
LANES = 128
LOADS = 2
CHUNKS = 4
SENDER, SOLVER = 1, 0
VMEM = pl.BlockSpec(memory_space=pltpu.VMEM)
HBM = pl.BlockSpec(memory_space=pltpu.HBM)


def pieces_of(value):
    high = value.astype(jnp.bfloat16).astype(jnp.float32)
    rest = value - high
    middle = rest.astype(jnp.bfloat16).astype(jnp.float32)
    low = (rest - middle).astype(jnp.bfloat16).astype(jnp.float32)
    return high, middle, low


def stacked(*rows):
    rows += (jnp.zeros_like(rows[0]),) * (-len(rows) % (16 // RANK))
    return jnp.concatenate(rows, axis=0).astype(jnp.bfloat16)


def unstacked_sum(products):
    return products[:RANK] + (products[RANK : 2 * RANK] + products[2 * RANK : 3 * RANK])


def to_blocks(ref, value):
    for block in range(value.shape[1] // LANES):
        ref[block * RANK : (block + 1) * RANK, :] = value[:, block * LANES : (block + 1) * LANES]


def from_blocks(value):
    blocks = [value[row : row + RANK] for row in range(0, value.shape[0], RANK)]
    return jnp.concatenate(blocks, axis=1)


def inverse_root(value):
    root = lax.rsqrt(value)
    return root * (1.5 - 0.5 * value * root * root)


def inverse_columns(gram):
    shape = (RANK, LANES)
    lower, inverse = {}, {}
    for i in range(RANK):
        for j in range(i + 1):
            rest = jnp.broadcast_to(gram[i : i + 1, j : j + 1], shape)
            for k in range(j):
                rest = rest - lower[i, k] * lower[j, k]
            if j < i:
                lower[i, j] = rest * inverse[j, j]
            else:
                inverse[i, i] = inverse_root(rest)
    for i in range(RANK):
        for j in range(i):
            total = lower[i, j] * inverse[j, j]
            for k in range(j + 1, i):
                total = total + lower[i, k] * inverse[k, j]
            inverse[i, j] = -total * inverse[i, i]
    row = lax.broadcasted_iota(jnp.int32, shape, 0)
    columns = []
    for j in range(RANK):
        column = jnp.zeros(shape, jnp.float32)
        for i in range(j, RANK):
            column = jnp.where(row == i, inverse[i, j], column)
        columns.append(column)
    return columns


def multiplied(columns, block):
    total = columns[0] * block[:1]
    for j in range(1, RANK):
        total = total + columns[j] * block[j : j + 1]
    return total


def left_kernel(q_hbm, grads_hbm, errors_hbm, left_ref, grads_ref, errors_ref, q_ref, q_sem, sems):
    rows, cols = grads_ref.shape
    step = rows // LOADS
    q_copy = pltpu.make_async_copy(q_hbm, q_ref, q_sem)
    q_copy.start()
    copies = []
    for chunk in range(LOADS):
        part = pl.ds(chunk * step, step)
        for which, (source, target) in enumerate(((grads_hbm, grads_ref), (errors_hbm, errors_ref))):
            copy = pltpu.make_async_copy(source.at[0, part, :], target.at[part, :], sems.at[chunk, which])
            copy.start()
            copies.append(copy)
    q_copy.wait()
    q = stacked(*pieces_of(q_ref[...]))
    total = jnp.zeros((q.shape[0], cols), jnp.float32)
    for chunk in range(LOADS):
        part = pl.ds(chunk * step, step)
        for which, source in enumerate((grads_ref, errors_ref)):
            copies[2 * chunk + which].wait()
            total += jnp.dot(
                q[:, chunk * step : (chunk + 1) * step], source[part, :], preferred_element_type=jnp.float32
            )
    to_blocks(left_ref, unstacked_sum(total))


def back_kernel(replicas, parts_ref, grads_ref, errors_ref, left_ref, terms_ref):
    left = from_blocks(jnp.sum(parts_ref[...], axis=0)) * (1.0 / replicas)
    left_ref[...] = left
    stack = stacked(*pieces_of(left))
    across = (((1,), (1,)), ((), ()))
    total = lax.dot_general(stack, grads_ref[...], across, preferred_element_type=jnp.float32)
    total += lax.dot_general(stack, errors_ref[...], across, preferred_element_type=jnp.float32)
    back = unstacked_sum(total)
    gram = lax.dot_general(
        left, left, across, precision=lax.Precision.HIGHEST, preferred_element_type=jnp.float32
    )
    used = back.shape[1] // LANES * RANK
    to_blocks(terms_ref, back)
    terms_ref[used:, :] = jnp.zeros((terms_ref.shape[0] - used, LANES), jnp.float32)
    terms_ref[used : used + RANK, :RANK] = gram


def sum_kernel(parts_ref, out_ref):
    used = parts_ref.shape[1]
    out_ref[:used, :] = jnp.sum(parts_ref[...], axis=0)
    out_ref[used:, :] = jnp.zeros((out_ref.shape[0] - used, LANES), jnp.float32)


def inverse_kernel(parts_ref, out_ref):
    used = out_ref.shape[0] - RANK * RANK
    out_ref[:used, :] = jnp.zeros((used, LANES), jnp.float32)
    columns = inverse_columns(jnp.sum(parts_ref[...], axis=0)[:RANK])
    for j, column in enumerate(columns):
        out_ref[used + j * RANK : used + (j + 1) * RANK, :] = column


def error_kernel(
    replicas, terms_ref, left_ref, grads_ref, errors_ref, out_hbm, right_hbm, q_hbm, out_ref, right_ref, q_ref, sems
):
    rows, cols = grads_ref.shape
    used = rows // LANES * RANK
    inverse = [terms_ref[SOLVER, used + j * RANK : used + (j + 1) * RANK, :] for j in range(RANK)]
    right = jnp.concatenate(
        [multiplied(inverse, left_ref[:, start : start + LANES]) for start in range(0, cols, LANES)], axis=1
    )
    new_q = jnp.concatenate(
        [multiplied(inverse, terms_ref[SENDER, start : start + RANK, :]) for start in range(0, used, RANK)], axis=1
    ) * (1.0 / replicas)
    right_ref[...] = right * math.sqrt(COLS)
    q_ref[...] = new_q
    copies = [
        pltpu.make_async_copy(right_ref, right_hbm, sems.at[CHUNKS]),
        pltpu.make_async_copy(q_ref, q_hbm, sems.at[CHUNKS + 1]),
    ]
    for copy in copies:
        copy.start()
    q1, q2, q3 = pieces_of(new_q)
    r1, r2, r3 = pieces_of(right)
    tall = stacked(q1, q1, q2, q2, q1, q3)
    wide = stacked(r1, r2, r1, r2, r3, r1)
    step = rows // CHUNKS
    for chunk in range(CHUNKS):
        part = pl.ds(chunk * step, step)
        approx = lax.dot_general(
            tall[:, chunk * step : (chunk + 1) * step],
            wide,
            (((0,), (0,)), ((), ())),
            preferred_element_type=jnp.float32,
        )
        merged = grads_ref[part, :].astype(jnp.float32) + errors_ref[part, :].astype(jnp.float32)
        out_ref[part, :] = (merged - approx).astype(jnp.bfloat16)
        copy = pltpu.make_async_copy(out_ref.at[part, :], out_hbm.at[0, part, :], sems.at[chunk])
        copy.start()
        copies.append(copy)
    for copy in copies:
        copy.wait()


def copies_for(value, axis):
    return jnp.broadcast_to(value[None], (lax.axis_size(axis),) + value.shape)


def exchange(value, axis):
    return lax.all_to_all(copies_for(value, axis), axis, 0, 0, tiled=True)


def on_device(grads, errors, q_in):
    replicas = lax.axis_size("z") * lax.axis_size("x")
    _, rows, cols = grads.shape
    f32, bf16 = jnp.float32, jnp.bfloat16
    left_rows, back_rows = RANK * cols // LANES, RANK * rows // LANES
    limit = pltpu.CompilerParams(vmem_limit_bytes=32 * 2**20)
    q_in, core = lax.optimization_barrier((q_in, lax.axis_index("core")))

    left, grads_near, errors_near = pl.pallas_call(
        left_kernel,
        out_shape=(
            pltpu.VMEM((left_rows, LANES), f32),
            pltpu.VMEM((rows, cols), bf16),
            pltpu.VMEM((rows, cols), bf16),
        ),
        in_specs=[HBM] * 3,
        out_specs=(VMEM, VMEM, VMEM),
        scratch_shapes=[pltpu.VMEM((RANK, rows), f32), pltpu.SemaphoreType.DMA, pltpu.SemaphoreType.DMA((LOADS, 2))],
        compiler_params=limit,
        name="left",
    )(*(pltpu.with_memory_space_constraint(x, pltpu.HBM) for x in (q_in.T, grads, errors)))

    left = jnp.sum(exchange(left, "x"), axis=0)
    left, terms = pl.pallas_call(
        functools.partial(back_kernel, replicas),
        out_shape=(
            pltpu.VMEM((RANK, cols), f32),
            pltpu.VMEM((back_rows + 8, LANES), f32),
        ),
        in_specs=[VMEM] * 3,
        out_specs=(VMEM, VMEM),
        compiler_params=limit,
        name="back",
    )(exchange(left, "z"), grads_near, errors_near)

    terms = jnp.sum(lax.all_gather(terms, "core"), axis=0)

    def place(kernel, parts, name):
        shape = pltpu.VMEM((back_rows + RANK * RANK, LANES), f32)
        return pl.pallas_call(
            kernel, out_shape=shape, in_specs=[VMEM], out_specs=VMEM, compiler_params=limit, name=name
        )(parts)

    def sum_back(terms):
        back = jnp.sum(exchange(terms[:back_rows], "y"), axis=0)
        back = jnp.sum(exchange(back, "x"), axis=0)
        return place(sum_kernel, exchange(back, "z"), "sum")

    def invert_gram(terms):
        return place(inverse_kernel, exchange(terms[back_rows:], "y"), "inverse")

    terms, core = lax.optimization_barrier((terms, core))
    terms = lax.cond(core == SENDER, sum_back, invert_gram, terms)
    terms = lax.all_gather(terms, "core")

    new_error, right_factor, new_q = pl.pallas_call(
        functools.partial(error_kernel, replicas),
        out_shape=(
            jax.ShapeDtypeStruct((1, rows, cols), bf16),
            jax.ShapeDtypeStruct((RANK, cols), f32),
            jax.ShapeDtypeStruct((RANK, rows), f32),
        ),
        in_specs=[VMEM] * 4,
        out_specs=(HBM, HBM, HBM),
        scratch_shapes=[
            pltpu.VMEM((rows, cols), bf16),
            pltpu.VMEM((RANK, cols), f32),
            pltpu.VMEM((RANK, rows), f32),
            pltpu.SemaphoreType.DMA((CHUNKS + 2,)),
        ],
        compiler_params=limit,
        name="error",
    )(terms, left, grads_near, errors_near)
    return new_error, right_factor.T, new_q.T


def solution(mesh):
    physical = Mesh(mesh.devices.reshape(8, 8, 8, 2), ("z", "x", "y", "core"))
    dp, tensor = ("z", "x"), ("y", "core")
    return jax.shard_map(
        on_device,
        mesh=physical,
        in_specs=(P(dp, None, tensor), P(dp, None, tensor), P()),
        out_specs=(P(dp, None, tensor), P(tensor, None), P()),
        check_vma=False,
    )
```

```python
import functools
import math

import jax
import jax.numpy as jnp
from jax import lax
from jax.experimental import pallas as pl
from jax.experimental.pallas import tpu as pltpu
from jax.sharding import Mesh
from jax.sharding import PartitionSpec as P

COLS = 8192
RANK = 4
LANES = 128
LOADS = 2
CHUNKS = 4
SENDER, SOLVER = 1, 0
FEWER = 8
VMEM = pl.BlockSpec(memory_space=pltpu.VMEM)
HBM = pl.BlockSpec(memory_space=pltpu.HBM)


def pieces_of(value):
    high = value.astype(jnp.bfloat16).astype(jnp.float32)
    rest = value - high
    middle = rest.astype(jnp.bfloat16).astype(jnp.float32)
    low = (rest - middle).astype(jnp.bfloat16).astype(jnp.float32)
    return high, middle, low


def stacked(*rows):
    rows += (jnp.zeros_like(rows[0]),) * (-len(rows) % (16 // RANK))
    return jnp.concatenate(rows, axis=0).astype(jnp.bfloat16)


def unstacked_sum(products):
    return products[:RANK] + (products[RANK : 2 * RANK] + products[2 * RANK : 3 * RANK])


def to_blocks(ref, value):
    for block in range(value.shape[1] // LANES):
        ref[block * RANK : (block + 1) * RANK, :] = value[:, block * LANES : (block + 1) * LANES]


def from_blocks(value):
    blocks = [value[row : row + RANK] for row in range(0, value.shape[0], RANK)]
    return jnp.concatenate(blocks, axis=1)


def inverse_root(value):
    root = lax.rsqrt(value)
    return root * (1.5 - 0.5 * value * root * root)


def inverse_columns(gram):
    shape = (RANK, LANES)
    lower, inverse = {}, {}
    for i in range(RANK):
        for j in range(i + 1):
            rest = jnp.broadcast_to(gram[i : i + 1, j : j + 1], shape)
            for k in range(j):
                rest = rest - lower[i, k] * lower[j, k]
            if j < i:
                lower[i, j] = rest * inverse[j, j]
            else:
                inverse[i, i] = inverse_root(rest)
    for i in range(RANK):
        for j in range(i):
            total = lower[i, j] * inverse[j, j]
            for k in range(j + 1, i):
                total = total + lower[i, k] * inverse[k, j]
            inverse[i, j] = -total * inverse[i, i]
    row = lax.broadcasted_iota(jnp.int32, shape, 0)
    columns = []
    for j in range(RANK):
        column = jnp.zeros(shape, jnp.float32)
        for i in range(j, RANK):
            column = jnp.where(row == i, inverse[i, j], column)
        columns.append(column)
    return columns


def multiplied(columns, block):
    total = columns[0] * block[:1]
    for j in range(1, RANK):
        total = total + columns[j] * block[j : j + 1]
    return total


def left_kernel(q_hbm, grads_hbm, errors_hbm, left_ref, grads_ref, errors_ref, q_ref, q_sem, sems):
    rows, cols = grads_ref.shape
    step = rows // LOADS
    q_copy = pltpu.make_async_copy(q_hbm, q_ref, q_sem)
    q_copy.start()
    copies = []
    for chunk in range(LOADS):
        part = pl.ds(chunk * step, step)
        for which, (source, target) in enumerate(((grads_hbm, grads_ref), (errors_hbm, errors_ref))):
            copy = pltpu.make_async_copy(source.at[0, part, :], target.at[part, :], sems.at[chunk, which])
            copy.start()
            copies.append(copy)
    q_copy.wait()
    q = stacked(*pieces_of(q_ref[...]))
    total = jnp.zeros((q.shape[0], cols), jnp.float32)
    for chunk in range(LOADS):
        part = pl.ds(chunk * step, step)
        for which, source in enumerate((grads_ref, errors_ref)):
            copies[2 * chunk + which].wait()
            total += jnp.dot(
                q[:, chunk * step : (chunk + 1) * step], source[part, :], preferred_element_type=jnp.float32
            )
    to_blocks(left_ref, unstacked_sum(total))


def back_kernel(replicas, parts_ref, grads_ref, errors_ref, left_ref, terms_ref):
    left = from_blocks(jnp.sum(parts_ref[...], axis=0)) * (1.0 / replicas)
    left_ref[...] = left
    stack = stacked(*pieces_of(left))
    across = (((1,), (1,)), ((), ()))
    total = lax.dot_general(stack, grads_ref[...], across, preferred_element_type=jnp.float32)
    total += lax.dot_general(stack, errors_ref[...], across, preferred_element_type=jnp.float32)
    back = unstacked_sum(total)
    gram = lax.dot_general(
        left, left, across, precision=lax.Precision.HIGHEST, preferred_element_type=jnp.float32
    )
    used = back.shape[1] // LANES * RANK
    to_blocks(terms_ref, back)
    terms_ref[used:, :] = jnp.zeros((terms_ref.shape[0] - used, LANES), jnp.float32)
    terms_ref[used : used + RANK, :RANK] = gram


def inverse_kernel(replicas, parts_ref, out_ref):
    terms = jnp.sum(parts_ref[...], axis=0)
    out_ref[:FEWER, :] = terms[:FEWER]
    columns = inverse_columns(terms[FEWER : FEWER + RANK] * (1.0 / replicas))
    for j, column in enumerate(columns):
        out_ref[FEWER + j * RANK : FEWER + (j + 1) * RANK, :] = column


def error_kernel(
    replicas, terms_ref, left_ref, grads_ref, errors_ref, out_hbm, right_hbm, q_hbm, out_ref, right_ref, q_ref, sems
):
    rows, cols = grads_ref.shape
    inverse = [terms_ref[SOLVER, start : start + RANK, :] for start in range(FEWER, FEWER + RANK * RANK, RANK)]
    more = rows // LANES * RANK - FEWER
    blocks = [terms_ref[SENDER, start : start + RANK, :] for start in range(0, more, RANK)]
    blocks += [terms_ref[SOLVER, start : start + RANK, :] for start in range(0, FEWER, RANK)]
    right = jnp.concatenate(
        [multiplied(inverse, left_ref[:, start : start + LANES]) for start in range(0, cols, LANES)], axis=1
    )
    new_q = jnp.concatenate([multiplied(inverse, block) for block in blocks], axis=1) * (1.0 / replicas)
    right_ref[...] = right * math.sqrt(COLS)
    q_ref[...] = new_q
    copies = [
        pltpu.make_async_copy(right_ref, right_hbm, sems.at[CHUNKS]),
        pltpu.make_async_copy(q_ref, q_hbm, sems.at[CHUNKS + 1]),
    ]
    for copy in copies:
        copy.start()
    q1, q2, q3 = pieces_of(new_q)
    r1, r2, r3 = pieces_of(right)
    tall = stacked(q1, q1, q2, q2, q1, q3)
    wide = stacked(r1, r2, r1, r2, r3, r1)
    step = rows // CHUNKS
    for chunk in range(CHUNKS):
        part = pl.ds(chunk * step, step)
        approx = lax.dot_general(
            tall[:, chunk * step : (chunk + 1) * step],
            wide,
            (((0,), (0,)), ((), ())),
            preferred_element_type=jnp.float32,
        )
        merged = grads_ref[part, :].astype(jnp.float32) + errors_ref[part, :].astype(jnp.float32)
        out_ref[part, :] = (merged - approx).astype(jnp.bfloat16)
        copy = pltpu.make_async_copy(out_ref.at[part, :], out_hbm.at[0, part, :], sems.at[chunk])
        copy.start()
        copies.append(copy)
    for copy in copies:
        copy.wait()


def exchange(value, axes):
    peers = math.prod(lax.axis_size(axis) for axis in axes)
    copies = jnp.broadcast_to(value[None], (peers,) + value.shape)
    return lax.all_to_all(copies, axes, 0, 0, tiled=True)


def on_device(grads, errors, q_in):
    replicas = lax.axis_size("z") * lax.axis_size("x")
    _, rows, cols = grads.shape
    f32, bf16 = jnp.float32, jnp.bfloat16
    left_rows, back_rows = RANK * cols // LANES, RANK * rows // LANES
    limit = pltpu.CompilerParams(vmem_limit_bytes=32 * 2**20)
    q_in, core = lax.optimization_barrier((q_in, lax.axis_index("core")))

    left, grads_near, errors_near = pl.pallas_call(
        left_kernel,
        out_shape=(
            pltpu.VMEM((left_rows, LANES), f32),
            pltpu.VMEM((rows, cols), bf16),
            pltpu.VMEM((rows, cols), bf16),
        ),
        in_specs=[HBM] * 3,
        out_specs=(VMEM, VMEM, VMEM),
        scratch_shapes=[pltpu.VMEM((RANK, rows), f32), pltpu.SemaphoreType.DMA, pltpu.SemaphoreType.DMA((LOADS, 2))],
        compiler_params=limit,
        name="left",
    )(*(pltpu.with_memory_space_constraint(x, pltpu.HBM) for x in (q_in.T, grads, errors)))

    left = jnp.sum(exchange(left, ("x",)), axis=0)
    left, terms = pl.pallas_call(
        functools.partial(back_kernel, replicas),
        out_shape=(
            pltpu.VMEM((RANK, cols), f32),
            pltpu.VMEM((back_rows + 8, LANES), f32),
        ),
        in_specs=[VMEM] * 3,
        out_specs=(VMEM, VMEM),
        compiler_params=limit,
        name="back",
    )(exchange(left, ("z",)), grads_near, errors_near)

    terms = jnp.sum(lax.all_gather(terms, "core"), axis=0)

    near, far = ("x", "y_low"), ("z", "y_high")

    def most(terms):
        back = jnp.sum(exchange(terms[: back_rows - FEWER], near), axis=0)
        return jnp.sum(exchange(back, far), axis=0)

    def rest_and_inverse(terms):
        terms = jnp.sum(exchange(terms[back_rows - FEWER :], far), axis=0)
        return pl.pallas_call(
            functools.partial(inverse_kernel, replicas),
            out_shape=pltpu.VMEM((FEWER + RANK * RANK, LANES), f32),
            in_specs=[VMEM],
            out_specs=VMEM,
            compiler_params=limit,
            name="inverse",
        )(exchange(terms, near))

    terms, core = lax.optimization_barrier((terms, core))
    terms = lax.cond(core == SENDER, most, rest_and_inverse, terms)
    terms = lax.all_gather(terms, "core")

    new_error, right_factor, new_q = pl.pallas_call(
        functools.partial(error_kernel, replicas),
        out_shape=(
            jax.ShapeDtypeStruct((1, rows, cols), bf16),
            jax.ShapeDtypeStruct((RANK, cols), f32),
            jax.ShapeDtypeStruct((RANK, rows), f32),
        ),
        in_specs=[VMEM] * 4,
        out_specs=(HBM, HBM, HBM),
        scratch_shapes=[
            pltpu.VMEM((rows, cols), bf16),
            pltpu.VMEM((RANK, cols), f32),
            pltpu.VMEM((RANK, rows), f32),
            pltpu.SemaphoreType.DMA((CHUNKS + 2,)),
        ],
        compiler_params=limit,
        name="error",
    )(terms, left, grads_near, errors_near)
    return new_error, right_factor.T, new_q.T


def solution(mesh):
    physical = Mesh(mesh.devices.reshape(8, 8, 4, 2, 2), ("z", "x", "y_high", "y_low", "core"))
    dp, tensor = ("z", "x"), ("y_high", "y_low", "core")
    return jax.shard_map(
        on_device,
        mesh=physical,
        in_specs=(P(dp, None, tensor), P(dp, None, tensor), P()),
        out_specs=(P(dp, None, tensor), P(tensor, None), P()),
        check_vma=False,
    )
```

```python
import functools
import math

import jax
import jax.numpy as jnp
from jax import lax
from jax.experimental import pallas as pl
from jax.experimental.pallas import tpu as pltpu
from jax.sharding import Mesh
from jax.sharding import PartitionSpec as P

COLS = 8192
RANK = 4
LANES = 128
LOADS = 2
CHUNKS = 4
SENDER, SOLVER = 1, 0
FEWER = 8
VMEM = pl.BlockSpec(memory_space=pltpu.VMEM)
HBM = pl.BlockSpec(memory_space=pltpu.HBM)


def pieces_of(value):
    high = value.astype(jnp.bfloat16).astype(jnp.float32)
    rest = value - high
    middle = rest.astype(jnp.bfloat16).astype(jnp.float32)
    low = (rest - middle).astype(jnp.bfloat16).astype(jnp.float32)
    return high, middle, low


def stacked(*rows):
    rows += (jnp.zeros_like(rows[0]),) * (-len(rows) % (16 // RANK))
    return jnp.concatenate(rows, axis=0).astype(jnp.bfloat16)


def unstacked_sum(products):
    return products[:RANK] + (products[RANK : 2 * RANK] + products[2 * RANK : 3 * RANK])


def to_blocks(ref, value):
    for block in range(value.shape[1] // LANES):
        ref[block * RANK : (block + 1) * RANK, :] = value[:, block * LANES : (block + 1) * LANES]


def from_blocks(value):
    blocks = [value[row : row + RANK] for row in range(0, value.shape[0], RANK)]
    return jnp.concatenate(blocks, axis=1)


def inverse_root(value):
    root = lax.rsqrt(value)
    return root * (1.5 - 0.5 * value * root * root)


def inverse_columns(gram):
    shape = (RANK, LANES)
    lower, inverse = {}, {}
    for i in range(RANK):
        for j in range(i + 1):
            rest = jnp.broadcast_to(gram[i : i + 1, j : j + 1], shape)
            for k in range(j):
                rest = rest - lower[i, k] * lower[j, k]
            if j < i:
                lower[i, j] = rest * inverse[j, j]
            else:
                inverse[i, i] = inverse_root(rest)
    for i in range(RANK):
        for j in range(i):
            total = lower[i, j] * inverse[j, j]
            for k in range(j + 1, i):
                total = total + lower[i, k] * inverse[k, j]
            inverse[i, j] = -total * inverse[i, i]
    row = lax.broadcasted_iota(jnp.int32, shape, 0)
    columns = []
    for j in range(RANK):
        column = jnp.zeros(shape, jnp.float32)
        for i in range(j, RANK):
            column = jnp.where(row == i, inverse[i, j], column)
        columns.append(column)
    return columns


def multiplied(columns, block):
    total = columns[0] * block[:1]
    for j in range(1, RANK):
        total = total + columns[j] * block[j : j + 1]
    return total


def left_kernel(q_hbm, grads_hbm, errors_hbm, left_ref, grads_ref, errors_ref, q_ref, q_sem, sems):
    rows, cols = grads_ref.shape
    step = rows // LOADS
    q_copy = pltpu.make_async_copy(q_hbm, q_ref, q_sem)
    q_copy.start()
    copies = []
    for chunk in range(LOADS):
        part = pl.ds(chunk * step, step)
        for which, (source, target) in enumerate(((grads_hbm, grads_ref), (errors_hbm, errors_ref))):
            copy = pltpu.make_async_copy(source.at[0, part, :], target.at[part, :], sems.at[chunk, which])
            copy.start()
            copies.append(copy)
    q_copy.wait()
    q = stacked(*pieces_of(q_ref[...]))
    total = jnp.zeros((q.shape[0], cols), jnp.float32)
    for chunk in range(LOADS):
        part = pl.ds(chunk * step, step)
        for which, source in enumerate((grads_ref, errors_ref)):
            copies[2 * chunk + which].wait()
            total += jnp.dot(
                q[:, chunk * step : (chunk + 1) * step], source[part, :], preferred_element_type=jnp.float32
            )
    to_blocks(left_ref, unstacked_sum(total))


def back_kernel(replicas, parts_ref, grads_ref, errors_ref, left_ref, terms_ref):
    left = from_blocks(jnp.sum(parts_ref[...], axis=0)) * (1.0 / replicas)
    left_ref[...] = left
    stack = stacked(*pieces_of(left))
    across = (((1,), (1,)), ((), ()))
    total = lax.dot_general(stack, grads_ref[...], across, preferred_element_type=jnp.float32)
    total += lax.dot_general(stack, errors_ref[...], across, preferred_element_type=jnp.float32)
    back = unstacked_sum(total)
    gram = lax.dot_general(
        left, left, across, precision=lax.Precision.HIGHEST, preferred_element_type=jnp.float32
    )
    used = back.shape[1] // LANES * RANK
    to_blocks(terms_ref, back)
    terms_ref[used:, :] = jnp.zeros((terms_ref.shape[0] - used, LANES), jnp.float32)
    terms_ref[used : used + RANK, :RANK] = gram


def inverse_kernel(replicas, parts_ref, out_ref):
    terms = jnp.sum(parts_ref[...], axis=0)
    out_ref[:FEWER, :] = terms[:FEWER]
    columns = inverse_columns(terms[FEWER : FEWER + RANK] * (1.0 / replicas))
    for j, column in enumerate(columns):
        out_ref[FEWER + j * RANK : FEWER + (j + 1) * RANK, :] = column


def error_kernel(
    replicas, terms_ref, left_ref, grads_ref, errors_ref, out_hbm, right_hbm, q_hbm, out_ref, right_ref, q_ref, sems
):
    rows, cols = grads_ref.shape
    inverse = [terms_ref[SOLVER, start : start + RANK, :] for start in range(FEWER, FEWER + RANK * RANK, RANK)]
    more = rows // LANES * RANK - FEWER
    blocks = [terms_ref[SENDER, start : start + RANK, :] for start in range(0, more, RANK)]
    blocks += [terms_ref[SOLVER, start : start + RANK, :] for start in range(0, FEWER, RANK)]
    right = jnp.concatenate(
        [multiplied(inverse, left_ref[:, start : start + LANES]) for start in range(0, cols, LANES)], axis=1
    )
    new_q = jnp.concatenate([multiplied(inverse, block) for block in blocks], axis=1) * (1.0 / replicas)
    right_ref[...] = right * math.sqrt(COLS)
    q_ref[...] = new_q
    copies = [
        pltpu.make_async_copy(right_ref, right_hbm, sems.at[CHUNKS]),
        pltpu.make_async_copy(q_ref, q_hbm, sems.at[CHUNKS + 1]),
    ]
    for copy in copies:
        copy.start()
    q1, q2, q3 = pieces_of(new_q)
    r1, r2, r3 = pieces_of(right)
    tall = stacked(q1, q1, q2, q2, q1, q3)
    wide = stacked(r1, r2, r1, r2, r3, r1)
    step = rows // CHUNKS
    for chunk in range(CHUNKS):
        part = pl.ds(chunk * step, step)
        approx = lax.dot_general(
            tall[:, chunk * step : (chunk + 1) * step],
            wide,
            (((0,), (0,)), ((), ())),
            preferred_element_type=jnp.float32,
        )
        merged = grads_ref[part, :].astype(jnp.float32) + errors_ref[part, :].astype(jnp.float32)
        out_ref[part, :] = (merged - approx).astype(jnp.bfloat16)
        copy = pltpu.make_async_copy(out_ref.at[part, :], out_hbm.at[0, part, :], sems.at[chunk])
        copy.start()
        copies.append(copy)
    for copy in copies:
        copy.wait()


def exchange(value, axes):
    peers = math.prod(lax.axis_size(axis) for axis in axes)
    copies = jnp.broadcast_to(value[None], (peers,) + value.shape)
    return lax.all_to_all(copies, axes, 0, 0, tiled=True)


def on_device(grads, errors, q_in):
    replicas = math.prod(lax.axis_size(axis) for axis in ("z", "x_high", "x_low"))
    _, rows, cols = grads.shape
    f32, bf16 = jnp.float32, jnp.bfloat16
    left_rows, back_rows = RANK * cols // LANES, RANK * rows // LANES
    limit = pltpu.CompilerParams(vmem_limit_bytes=32 * 2**20)
    q_in, core = lax.optimization_barrier((q_in, lax.axis_index("core")))

    left, grads_near, errors_near = pl.pallas_call(
        left_kernel,
        out_shape=(
            pltpu.VMEM((left_rows, LANES), f32),
            pltpu.VMEM((rows, cols), bf16),
            pltpu.VMEM((rows, cols), bf16),
        ),
        in_specs=[HBM] * 3,
        out_specs=(VMEM, VMEM, VMEM),
        scratch_shapes=[pltpu.VMEM((RANK, rows), f32), pltpu.SemaphoreType.DMA, pltpu.SemaphoreType.DMA((LOADS, 2))],
        compiler_params=limit,
        name="left",
    )(*(pltpu.with_memory_space_constraint(x, pltpu.HBM) for x in (q_in.T, grads, errors)))

    left = jnp.sum(exchange(left, ("x_high", "x_low")), axis=0)
    left, terms = pl.pallas_call(
        functools.partial(back_kernel, replicas),
        out_shape=(
            pltpu.VMEM((RANK, cols), f32),
            pltpu.VMEM((back_rows + 8, LANES), f32),
        ),
        in_specs=[VMEM] * 3,
        out_specs=(VMEM, VMEM),
        compiler_params=limit,
        name="back",
    )(exchange(left, ("z",)), grads_near, errors_near)

    terms = jnp.sum(lax.all_gather(terms, "core"), axis=0)

    near, far = ("y", "x_low"), ("z", "x_high")

    def most(terms):
        back = jnp.sum(exchange(terms[: back_rows - FEWER], near), axis=0)
        return jnp.sum(exchange(back, far), axis=0)

    def rest_and_inverse(terms):
        terms = jnp.sum(exchange(terms[back_rows - FEWER :], far), axis=0)
        return pl.pallas_call(
            functools.partial(inverse_kernel, replicas),
            out_shape=pltpu.VMEM((FEWER + RANK * RANK, LANES), f32),
            in_specs=[VMEM],
            out_specs=VMEM,
            compiler_params=limit,
            name="inverse",
        )(exchange(terms, near))

    terms, core = lax.optimization_barrier((terms, core))
    terms = lax.cond(core == SENDER, most, rest_and_inverse, terms)
    terms = lax.all_gather(terms, "core")

    new_error, right_factor, new_q = pl.pallas_call(
        functools.partial(error_kernel, replicas),
        out_shape=(
            jax.ShapeDtypeStruct((1, rows, cols), bf16),
            jax.ShapeDtypeStruct((RANK, cols), f32),
            jax.ShapeDtypeStruct((RANK, rows), f32),
        ),
        in_specs=[VMEM] * 4,
        out_specs=(HBM, HBM, HBM),
        scratch_shapes=[
            pltpu.VMEM((rows, cols), bf16),
            pltpu.VMEM((RANK, cols), f32),
            pltpu.VMEM((RANK, rows), f32),
            pltpu.SemaphoreType.DMA((CHUNKS + 2,)),
        ],
        compiler_params=limit,
        name="error",
    )(terms, left, grads_near, errors_near)
    return new_error, right_factor.T, new_q.T


def solution(mesh):
    physical = Mesh(mesh.devices.reshape(8, 4, 2, 8, 2), ("z", "x_high", "x_low", "y", "core"))
    dp, tensor = ("z", "x_high", "x_low"), ("y", "core")
    return jax.shard_map(
        on_device,
        mesh=physical,
        in_specs=(P(dp, None, tensor), P(dp, None, tensor), P()),
        out_specs=(P(dp, None, tensor), P(tensor, None), P()),
        check_vma=False,
    )
```

```python
import functools
import math

import jax
import jax.numpy as jnp
from jax import lax
from jax.experimental import pallas as pl
from jax.experimental.pallas import tpu as pltpu
from jax.sharding import Mesh
from jax.sharding import PartitionSpec as P

COLS = 8192
RANK = 4
LANES = 128
LOADS = 2
CHUNKS = 4
SENDER, SOLVER = 1, 0
FEWER = 8
VMEM = pl.BlockSpec(memory_space=pltpu.VMEM)
HBM = pl.BlockSpec(memory_space=pltpu.HBM)


def pieces_of(value):
    high = value.astype(jnp.bfloat16).astype(jnp.float32)
    rest = value - high
    middle = rest.astype(jnp.bfloat16).astype(jnp.float32)
    low = (rest - middle).astype(jnp.bfloat16).astype(jnp.float32)
    return high, middle, low


def stacked(*rows):
    rows += (jnp.zeros_like(rows[0]),) * (-len(rows) % (16 // RANK))
    return jnp.concatenate(rows, axis=0).astype(jnp.bfloat16)


def unstacked_sum(products):
    return products[:RANK] + (products[RANK : 2 * RANK] + products[2 * RANK : 3 * RANK])


def to_blocks(ref, value):
    for block in range(value.shape[1] // LANES):
        ref[block * RANK : (block + 1) * RANK, :] = value[:, block * LANES : (block + 1) * LANES]


def from_blocks(value):
    blocks = [value[row : row + RANK] for row in range(0, value.shape[0], RANK)]
    return jnp.concatenate(blocks, axis=1)


def inverse_root(value):
    root = lax.rsqrt(value)
    return root * (1.5 - 0.5 * value * root * root)


def inverse_columns(gram):
    shape = (RANK, LANES)
    lower, inverse = {}, {}
    for i in range(RANK):
        for j in range(i + 1):
            rest = jnp.broadcast_to(gram[i : i + 1, j : j + 1], shape)
            for k in range(j):
                rest = rest - lower[i, k] * lower[j, k]
            if j < i:
                lower[i, j] = rest * inverse[j, j]
            else:
                inverse[i, i] = inverse_root(rest)
    for i in range(RANK):
        for j in range(i):
            total = lower[i, j] * inverse[j, j]
            for k in range(j + 1, i):
                total = total + lower[i, k] * inverse[k, j]
            inverse[i, j] = -total * inverse[i, i]
    row = lax.broadcasted_iota(jnp.int32, shape, 0)
    columns = []
    for j in range(RANK):
        column = jnp.zeros(shape, jnp.float32)
        for i in range(j, RANK):
            column = jnp.where(row == i, inverse[i, j], column)
        columns.append(column)
    return columns


def multiplied(columns, block):
    total = columns[0] * block[:1]
    for j in range(1, RANK):
        total = total + columns[j] * block[j : j + 1]
    return total


def left_kernel(q_hbm, grads_hbm, errors_hbm, left_ref, grads_ref, errors_ref, q_ref, q_sem, sems):
    rows, cols = grads_ref.shape
    step = rows // LOADS
    q_copy = pltpu.make_async_copy(q_hbm, q_ref, q_sem)
    q_copy.start()
    copies = []
    for chunk in range(LOADS):
        part = pl.ds(chunk * step, step)
        for which, (source, target) in enumerate(((grads_hbm, grads_ref), (errors_hbm, errors_ref))):
            copy = pltpu.make_async_copy(source.at[0, part, :], target.at[part, :], sems.at[chunk, which])
            copy.start()
            copies.append(copy)
    q_copy.wait()
    q = stacked(*pieces_of(q_ref[...]))
    total = jnp.zeros((q.shape[0], cols), jnp.float32)
    for chunk in range(LOADS):
        part = pl.ds(chunk * step, step)
        for which, source in enumerate((grads_ref, errors_ref)):
            copies[2 * chunk + which].wait()
            total += jnp.dot(
                q[:, chunk * step : (chunk + 1) * step], source[part, :], preferred_element_type=jnp.float32
            )
    to_blocks(left_ref, unstacked_sum(total))


def back_kernel(replicas, sum_ref, grads_ref, errors_ref, left_ref, terms_ref):
    left = from_blocks(sum_ref[...]) * (1.0 / replicas)
    left_ref[...] = left
    stack = stacked(*pieces_of(left))
    across = (((1,), (1,)), ((), ()))
    total = lax.dot_general(stack, grads_ref[...], across, preferred_element_type=jnp.float32)
    total += lax.dot_general(stack, errors_ref[...], across, preferred_element_type=jnp.float32)
    back = unstacked_sum(total)
    gram = lax.dot_general(
        left, left, across, precision=lax.Precision.HIGHEST, preferred_element_type=jnp.float32
    )
    used = back.shape[1] // LANES * RANK
    to_blocks(terms_ref, back)
    terms_ref[used:, :] = jnp.zeros((terms_ref.shape[0] - used, LANES), jnp.float32)
    terms_ref[used : used + RANK, :RANK] = gram


def inverse_kernel(replicas, parts_ref, out_ref):
    terms = jnp.sum(parts_ref[...], axis=0)
    out_ref[:FEWER, :] = terms[:FEWER]
    columns = inverse_columns(terms[FEWER : FEWER + RANK] * (1.0 / replicas))
    for j, column in enumerate(columns):
        out_ref[FEWER + j * RANK : FEWER + (j + 1) * RANK, :] = column


def error_kernel(
    replicas, terms_ref, left_ref, grads_ref, errors_ref, out_hbm, right_hbm, q_hbm, out_ref, right_ref, q_ref, sems
):
    rows, cols = grads_ref.shape
    inverse = [terms_ref[SOLVER, start : start + RANK, :] for start in range(FEWER, FEWER + RANK * RANK, RANK)]
    more = rows // LANES * RANK - FEWER
    blocks = [terms_ref[SENDER, start : start + RANK, :] for start in range(0, more, RANK)]
    blocks += [terms_ref[SOLVER, start : start + RANK, :] for start in range(0, FEWER, RANK)]
    right = jnp.concatenate(
        [multiplied(inverse, left_ref[:, start : start + LANES]) for start in range(0, cols, LANES)], axis=1
    )
    new_q = jnp.concatenate([multiplied(inverse, block) for block in blocks], axis=1) * (1.0 / replicas)
    right_ref[...] = right * math.sqrt(COLS)
    q_ref[...] = new_q
    copies = [
        pltpu.make_async_copy(right_ref, right_hbm, sems.at[CHUNKS]),
        pltpu.make_async_copy(q_ref, q_hbm, sems.at[CHUNKS + 1]),
    ]
    for copy in copies:
        copy.start()
    q1, q2, q3 = pieces_of(new_q)
    r1, r2, r3 = pieces_of(right)
    tall = stacked(q1, q1, q2, q2, q1, q3)
    wide = stacked(r1, r2, r1, r2, r3, r1)
    step = rows // CHUNKS
    for chunk in range(CHUNKS):
        part = pl.ds(chunk * step, step)
        approx = lax.dot_general(
            tall[:, chunk * step : (chunk + 1) * step],
            wide,
            (((0,), (0,)), ((), ())),
            preferred_element_type=jnp.float32,
        )
        merged = grads_ref[part, :].astype(jnp.float32) + errors_ref[part, :].astype(jnp.float32)
        out_ref[part, :] = (merged - approx).astype(jnp.bfloat16)
        copy = pltpu.make_async_copy(out_ref.at[part, :], out_hbm.at[0, part, :], sems.at[chunk])
        copy.start()
        copies.append(copy)
    for copy in copies:
        copy.wait()


def exchange(value, axes):
    peers = math.prod(lax.axis_size(axis) for axis in axes)
    copies = jnp.broadcast_to(value[None], (peers,) + value.shape)
    return lax.all_to_all(copies, axes, 0, 0, tiled=True)


def on_device(grads, errors, q_in):
    replicas = lax.axis_size("z") * lax.axis_size("x")
    _, rows, cols = grads.shape
    f32, bf16 = jnp.float32, jnp.bfloat16
    left_rows, back_rows = RANK * cols // LANES, RANK * rows // LANES
    limit = pltpu.CompilerParams(vmem_limit_bytes=32 * 2**20)
    q_in, core = lax.optimization_barrier((q_in, lax.axis_index("core")))

    left, grads_near, errors_near = pl.pallas_call(
        left_kernel,
        out_shape=(
            pltpu.VMEM((left_rows, LANES), f32),
            pltpu.VMEM((rows, cols), bf16),
            pltpu.VMEM((rows, cols), bf16),
        ),
        in_specs=[HBM] * 3,
        out_specs=(VMEM, VMEM, VMEM),
        scratch_shapes=[pltpu.VMEM((RANK, rows), f32), pltpu.SemaphoreType.DMA, pltpu.SemaphoreType.DMA((LOADS, 2))],
        compiler_params=limit,
        name="left",
    )(*(pltpu.with_memory_space_constraint(x, pltpu.HBM) for x in (q_in.T, grads, errors)))

    def in_two(left):
        left = jnp.sum(exchange(left, ("x",)), axis=0)
        return jnp.sum(exchange(left, ("z",)), axis=0)

    def in_one(left):
        return jnp.sum(exchange(left, ("z", "x")), axis=0)

    left, core = lax.optimization_barrier((left, core))
    left = lax.cond(core == SENDER, in_two, in_one, left)
    left, terms = pl.pallas_call(
        functools.partial(back_kernel, replicas),
        out_shape=(
            pltpu.VMEM((RANK, cols), f32),
            pltpu.VMEM((back_rows + 8, LANES), f32),
        ),
        in_specs=[VMEM] * 3,
        out_specs=(VMEM, VMEM),
        compiler_params=limit,
        name="back",
    )(left, grads_near, errors_near)

    terms = jnp.sum(lax.all_gather(terms, "core"), axis=0)

    near, far = ("x", "y_low"), ("z", "y_high")

    def most(terms):
        back = jnp.sum(exchange(terms[: back_rows - FEWER], near), axis=0)
        return jnp.sum(exchange(back, far), axis=0)

    def rest_and_inverse(terms):
        terms = jnp.sum(exchange(terms[back_rows - FEWER :], far), axis=0)
        return pl.pallas_call(
            functools.partial(inverse_kernel, replicas),
            out_shape=pltpu.VMEM((FEWER + RANK * RANK, LANES), f32),
            in_specs=[VMEM],
            out_specs=VMEM,
            compiler_params=limit,
            name="inverse",
        )(exchange(terms, near))

    terms, core = lax.optimization_barrier((terms, core))
    terms = lax.cond(core == SENDER, most, rest_and_inverse, terms)
    terms = lax.all_gather(terms, "core")

    new_error, right_factor, new_q = pl.pallas_call(
        functools.partial(error_kernel, replicas),
        out_shape=(
            jax.ShapeDtypeStruct((1, rows, cols), bf16),
            jax.ShapeDtypeStruct((RANK, cols), f32),
            jax.ShapeDtypeStruct((RANK, rows), f32),
        ),
        in_specs=[VMEM] * 4,
        out_specs=(HBM, HBM, HBM),
        scratch_shapes=[
            pltpu.VMEM((rows, cols), bf16),
            pltpu.VMEM((RANK, cols), f32),
            pltpu.VMEM((RANK, rows), f32),
            pltpu.SemaphoreType.DMA((CHUNKS + 2,)),
        ],
        compiler_params=limit,
        name="error",
    )(terms, left, grads_near, errors_near)
    return new_error, right_factor.T, new_q.T


def solution(mesh):
    physical = Mesh(mesh.devices.reshape(8, 8, 4, 2, 2), ("z", "x", "y_high", "y_low", "core"))
    dp, tensor = ("z", "x"), ("y_high", "y_low", "core")
    return jax.shard_map(
        on_device,
        mesh=physical,
        in_specs=(P(dp, None, tensor), P(dp, None, tensor), P()),
        out_specs=(P(dp, None, tensor), P(tensor, None), P()),
        check_vma=False,
    )
```

```python
import functools
import math

import jax
import jax.numpy as jnp
from jax import lax
from jax.experimental import pallas as pl
from jax.experimental.pallas import tpu as pltpu
from jax.sharding import Mesh
from jax.sharding import PartitionSpec as P

COLS = 8192
RANK = 4
LANES = 128
LOADS = 2
CHUNKS = 4
SENDER, SOLVER = 1, 0
FEWER = 8
VMEM = pl.BlockSpec(memory_space=pltpu.VMEM)
HBM = pl.BlockSpec(memory_space=pltpu.HBM)


def pieces_of(value):
    high = value.astype(jnp.bfloat16).astype(jnp.float32)
    rest = value - high
    middle = rest.astype(jnp.bfloat16).astype(jnp.float32)
    low = (rest - middle).astype(jnp.bfloat16).astype(jnp.float32)
    return high, middle, low


def stacked(*rows):
    rows += (jnp.zeros_like(rows[0]),) * (-len(rows) % (16 // RANK))
    return jnp.concatenate(rows, axis=0).astype(jnp.bfloat16)


def unstacked_sum(products):
    return products[:RANK] + (products[RANK : 2 * RANK] + products[2 * RANK : 3 * RANK])


def to_blocks(ref, value):
    for block in range(value.shape[1] // LANES):
        ref[block * RANK : (block + 1) * RANK, :] = value[:, block * LANES : (block + 1) * LANES]


def from_blocks(value):
    blocks = [value[row : row + RANK] for row in range(0, value.shape[0], RANK)]
    return jnp.concatenate(blocks, axis=1)


def inverse_root(value):
    root = lax.rsqrt(value)
    return root * (1.5 - 0.5 * value * root * root)


def inverse_columns(gram):
    shape = (RANK, LANES)
    lower, inverse = {}, {}
    for i in range(RANK):
        for j in range(i + 1):
            rest = jnp.broadcast_to(gram[i : i + 1, j : j + 1], shape)
            for k in range(j):
                rest = rest - lower[i, k] * lower[j, k]
            if j < i:
                lower[i, j] = rest * inverse[j, j]
            else:
                inverse[i, i] = inverse_root(rest)
    for i in range(RANK):
        for j in range(i):
            total = lower[i, j] * inverse[j, j]
            for k in range(j + 1, i):
                total = total + lower[i, k] * inverse[k, j]
            inverse[i, j] = -total * inverse[i, i]
    row = lax.broadcasted_iota(jnp.int32, shape, 0)
    columns = []
    for j in range(RANK):
        column = jnp.zeros(shape, jnp.float32)
        for i in range(j, RANK):
            column = jnp.where(row == i, inverse[i, j], column)
        columns.append(column)
    return columns


def multiplied(columns, block):
    total = columns[0] * block[:1]
    for j in range(1, RANK):
        total = total + columns[j] * block[j : j + 1]
    return total


def left_kernel(q_hbm, grads_hbm, errors_hbm, left_ref, grads_ref, errors_ref, q_ref, q_sem, sems):
    rows, cols = grads_ref.shape
    step = rows // LOADS
    q_copy = pltpu.make_async_copy(q_hbm, q_ref, q_sem)
    q_copy.start()
    copies = []
    for chunk in range(LOADS):
        part = pl.ds(chunk * step, step)
        for which, (source, target) in enumerate(((grads_hbm, grads_ref), (errors_hbm, errors_ref))):
            copy = pltpu.make_async_copy(source.at[0, part, :], target.at[part, :], sems.at[chunk, which])
            copy.start()
            copies.append(copy)
    q_copy.wait()
    q = stacked(*pieces_of(q_ref[...]))
    total = jnp.zeros((q.shape[0], cols), jnp.float32)
    for chunk in range(LOADS):
        part = pl.ds(chunk * step, step)
        for which, source in enumerate((grads_ref, errors_ref)):
            copies[2 * chunk + which].wait()
            total += jnp.dot(
                q[:, chunk * step : (chunk + 1) * step], source[part, :], preferred_element_type=jnp.float32
            )
    to_blocks(left_ref, unstacked_sum(total))


def back_kernel(replicas, sum_ref, grads_ref, errors_ref, left_ref, terms_ref):
    left = from_blocks(sum_ref[...]) * (1.0 / replicas)
    left_ref[...] = left
    stack = stacked(*pieces_of(left))
    across = (((1,), (1,)), ((), ()))
    total = lax.dot_general(stack, grads_ref[...], across, preferred_element_type=jnp.float32)
    total += lax.dot_general(stack, errors_ref[...], across, preferred_element_type=jnp.float32)
    back = unstacked_sum(total)
    gram = lax.dot_general(
        left, left, across, precision=lax.Precision.HIGHEST, preferred_element_type=jnp.float32
    )
    used = back.shape[1] // LANES * RANK
    to_blocks(terms_ref, back)
    terms_ref[used:, :] = jnp.zeros((terms_ref.shape[0] - used, LANES), jnp.float32)
    terms_ref[used : used + RANK, :RANK] = gram


def inverse_kernel(replicas, parts_ref, out_ref):
    terms = jnp.sum(parts_ref[...], axis=0)
    out_ref[:FEWER, :] = terms[:FEWER]
    columns = inverse_columns(terms[FEWER : FEWER + RANK] * (1.0 / replicas))
    for j, column in enumerate(columns):
        out_ref[FEWER + j * RANK : FEWER + (j + 1) * RANK, :] = column


def error_kernel(
    replicas, terms_ref, left_ref, grads_ref, errors_ref, out_hbm, right_hbm, q_hbm, out_ref, right_ref, q_ref, sems
):
    rows, cols = grads_ref.shape
    inverse = [terms_ref[SOLVER, start : start + RANK, :] for start in range(FEWER, FEWER + RANK * RANK, RANK)]
    more = rows // LANES * RANK - FEWER
    blocks = [terms_ref[SENDER, start : start + RANK, :] for start in range(0, more, RANK)]
    blocks += [terms_ref[SOLVER, start : start + RANK, :] for start in range(0, FEWER, RANK)]
    right = jnp.concatenate(
        [multiplied(inverse, left_ref[:, start : start + LANES]) for start in range(0, cols, LANES)], axis=1
    )
    new_q = jnp.concatenate([multiplied(inverse, block) for block in blocks], axis=1) * (1.0 / replicas)
    right_ref[...] = right * math.sqrt(COLS)
    q_ref[...] = new_q
    copies = [
        pltpu.make_async_copy(right_ref, right_hbm, sems.at[CHUNKS]),
        pltpu.make_async_copy(q_ref, q_hbm, sems.at[CHUNKS + 1]),
    ]
    for copy in copies:
        copy.start()
    q1, q2, q3 = pieces_of(new_q)
    r1, r2, r3 = pieces_of(right)
    tall = stacked(q1, q1, q2, q2, q1, q3)
    wide = stacked(r1, r2, r1, r2, r3, r1)
    step = rows // CHUNKS
    for chunk in range(CHUNKS):
        part = pl.ds(chunk * step, step)
        approx = lax.dot_general(
            tall[:, chunk * step : (chunk + 1) * step],
            wide,
            (((0,), (0,)), ((), ())),
            preferred_element_type=jnp.float32,
        )
        merged = grads_ref[part, :].astype(jnp.float32) + errors_ref[part, :].astype(jnp.float32)
        out_ref[part, :] = (merged - approx).astype(jnp.bfloat16)
        copy = pltpu.make_async_copy(out_ref.at[part, :], out_hbm.at[0, part, :], sems.at[chunk])
        copy.start()
        copies.append(copy)
    for copy in copies:
        copy.wait()


def exchange(value, axes):
    peers = math.prod(lax.axis_size(axis) for axis in axes)
    copies = jnp.broadcast_to(value[None], (peers,) + value.shape)
    return lax.all_to_all(copies, axes, 0, 0, tiled=True)


def on_device(grads, errors, q_in):
    replicas = lax.axis_size("z") * lax.axis_size("x")
    _, rows, cols = grads.shape
    f32, bf16 = jnp.float32, jnp.bfloat16
    left_rows, back_rows = RANK * cols // LANES, RANK * rows // LANES
    limit = pltpu.CompilerParams(vmem_limit_bytes=32 * 2**20)
    q_in, core = lax.optimization_barrier((q_in, lax.axis_index("core")))

    left, grads_near, errors_near = pl.pallas_call(
        left_kernel,
        out_shape=(
            pltpu.VMEM((left_rows, LANES), f32),
            pltpu.VMEM((rows, cols), bf16),
            pltpu.VMEM((rows, cols), bf16),
        ),
        in_specs=[HBM] * 3,
        out_specs=(VMEM, VMEM, VMEM),
        scratch_shapes=[pltpu.VMEM((RANK, rows), f32), pltpu.SemaphoreType.DMA, pltpu.SemaphoreType.DMA((LOADS, 2))],
        compiler_params=limit,
        name="left",
    )(*(pltpu.with_memory_space_constraint(x, pltpu.HBM) for x in (q_in.T, grads, errors)))

    def over(*axes):
        def sums(value):
            for axis in axes:
                value = jnp.sum(exchange(value, (axis,)), axis=0)
            return value

        return sums

    left, core = lax.optimization_barrier((left, core))
    left = lax.cond(core == SENDER, over("z", "x"), over("x", "z"), left)
    left, terms = pl.pallas_call(
        functools.partial(back_kernel, replicas),
        out_shape=(
            pltpu.VMEM((RANK, cols), f32),
            pltpu.VMEM((back_rows + 8, LANES), f32),
        ),
        in_specs=[VMEM] * 3,
        out_specs=(VMEM, VMEM),
        compiler_params=limit,
        name="back",
    )(left, grads_near, errors_near)

    terms = jnp.sum(lax.all_gather(terms, "core"), axis=0)

    near, far = ("x", "y_low"), ("z", "y_high")

    def most(terms):
        back = jnp.sum(exchange(terms[: back_rows - FEWER], near), axis=0)
        return jnp.sum(exchange(back, far), axis=0)

    def rest_and_inverse(terms):
        terms = jnp.sum(exchange(terms[back_rows - FEWER :], far), axis=0)
        return pl.pallas_call(
            functools.partial(inverse_kernel, replicas),
            out_shape=pltpu.VMEM((FEWER + RANK * RANK, LANES), f32),
            in_specs=[VMEM],
            out_specs=VMEM,
            compiler_params=limit,
            name="inverse",
        )(exchange(terms, near))

    terms, core = lax.optimization_barrier((terms, core))
    terms = lax.cond(core == SENDER, most, rest_and_inverse, terms)
    terms = lax.all_gather(terms, "core")

    new_error, right_factor, new_q = pl.pallas_call(
        functools.partial(error_kernel, replicas),
        out_shape=(
            jax.ShapeDtypeStruct((1, rows, cols), bf16),
            jax.ShapeDtypeStruct((RANK, cols), f32),
            jax.ShapeDtypeStruct((RANK, rows), f32),
        ),
        in_specs=[VMEM] * 4,
        out_specs=(HBM, HBM, HBM),
        scratch_shapes=[
            pltpu.VMEM((rows, cols), bf16),
            pltpu.VMEM((RANK, cols), f32),
            pltpu.VMEM((RANK, rows), f32),
            pltpu.SemaphoreType.DMA((CHUNKS + 2,)),
        ],
        compiler_params=limit,
        name="error",
    )(terms, left, grads_near, errors_near)
    return new_error, right_factor.T, new_q.T


def solution(mesh):
    physical = Mesh(mesh.devices.reshape(8, 8, 4, 2, 2), ("z", "x", "y_high", "y_low", "core"))
    dp, tensor = ("z", "x"), ("y_high", "y_low", "core")
    return jax.shard_map(
        on_device,
        mesh=physical,
        in_specs=(P(dp, None, tensor), P(dp, None, tensor), P()),
        out_specs=(P(dp, None, tensor), P(tensor, None), P()),
        check_vma=False,
    )
```

```python
import functools
import math

import jax
import jax.numpy as jnp
from jax import lax
from jax.experimental import pallas as pl
from jax.experimental.pallas import tpu as pltpu
from jax.sharding import Mesh
from jax.sharding import PartitionSpec as P

COLS = 8192
RANK = 4
LANES = 128
LOADS = 2
CHUNKS = 4
SENDER, SOLVER = 1, 0
FEWER = 2
VMEM = pl.BlockSpec(memory_space=pltpu.VMEM)
HBM = pl.BlockSpec(memory_space=pltpu.HBM)


def pieces_of(value):
    high = value.astype(jnp.bfloat16).astype(jnp.float32)
    rest = value - high
    middle = rest.astype(jnp.bfloat16).astype(jnp.float32)
    low = (rest - middle).astype(jnp.bfloat16).astype(jnp.float32)
    return high, middle, low


def stacked(*rows):
    rows += (jnp.zeros_like(rows[0]),) * (-len(rows) % (16 // RANK))
    return jnp.concatenate(rows, axis=0).astype(jnp.bfloat16)


def unstacked_sum(products):
    return products[:RANK] + (products[RANK : 2 * RANK] + products[2 * RANK : 3 * RANK])


def to_blocks(ref, value):
    for block in range(value.shape[1] // LANES):
        ref[block * RANK : (block + 1) * RANK, :] = value[:, block * LANES : (block + 1) * LANES]


def from_blocks(value):
    blocks = [value[row : row + RANK] for row in range(0, value.shape[0], RANK)]
    return jnp.concatenate(blocks, axis=1)


def inverse_root(value):
    root = lax.rsqrt(value)
    return root * (1.5 - 0.5 * value * root * root)


def inverse_columns(gram):
    shape = (RANK, LANES)
    lower, inverse = {}, {}
    for i in range(RANK):
        for j in range(i + 1):
            rest = jnp.broadcast_to(gram[i : i + 1, j : j + 1], shape)
            for k in range(j):
                rest = rest - lower[i, k] * lower[j, k]
            if j < i:
                lower[i, j] = rest * inverse[j, j]
            else:
                inverse[i, i] = inverse_root(rest)
    for i in range(RANK):
        for j in range(i):
            total = lower[i, j] * inverse[j, j]
            for k in range(j + 1, i):
                total = total + lower[i, k] * inverse[k, j]
            inverse[i, j] = -total * inverse[i, i]
    row = lax.broadcasted_iota(jnp.int32, shape, 0)
    columns = []
    for j in range(RANK):
        column = jnp.zeros(shape, jnp.float32)
        for i in range(j, RANK):
            column = jnp.where(row == i, inverse[i, j], column)
        columns.append(column)
    return columns


def multiplied(columns, block):
    total = columns[0] * block[:1]
    for j in range(1, RANK):
        total = total + columns[j] * block[j : j + 1]
    return total


def left_kernel(q_hbm, grads_hbm, errors_hbm, left_ref, grads_ref, errors_ref, q_ref, q_sem, sems):
    rows, cols = grads_ref.shape
    step = rows // LOADS
    q_copy = pltpu.make_async_copy(q_hbm, q_ref, q_sem)
    q_copy.start()
    copies = []
    for chunk in range(LOADS):
        part = pl.ds(chunk * step, step)
        for which, (source, target) in enumerate(((grads_hbm, grads_ref), (errors_hbm, errors_ref))):
            copy = pltpu.make_async_copy(source.at[0, part, :], target.at[part, :], sems.at[chunk, which])
            copy.start()
            copies.append(copy)
    q_copy.wait()
    q = stacked(*pieces_of(q_ref[...]))
    total = jnp.zeros((q.shape[0], cols), jnp.float32)
    for chunk in range(LOADS):
        part = pl.ds(chunk * step, step)
        for which, source in enumerate((grads_ref, errors_ref)):
            copies[2 * chunk + which].wait()
            total += jnp.dot(
                q[:, chunk * step : (chunk + 1) * step], source[part, :], preferred_element_type=jnp.float32
            )
    to_blocks(left_ref, unstacked_sum(total))


def back_kernel(replicas, parts_ref, grads_ref, errors_ref, left_ref, terms_ref):
    left = from_blocks(jnp.sum(parts_ref[...], axis=0)) * (1.0 / replicas)
    left_ref[...] = left
    stack = stacked(*pieces_of(left))
    across = (((1,), (1,)), ((), ()))
    total = lax.dot_general(stack, grads_ref[...], across, preferred_element_type=jnp.float32)
    total += lax.dot_general(stack, errors_ref[...], across, preferred_element_type=jnp.float32)
    back = unstacked_sum(total)
    gram = lax.dot_general(
        left, left, across, precision=lax.Precision.HIGHEST, preferred_element_type=jnp.float32
    )
    used = back.shape[1] // LANES
    for block in range(used):
        terms_ref[block] = back[:, block * LANES : (block + 1) * LANES]
    terms_ref[used] = jnp.zeros((RANK, LANES), jnp.float32)
    terms_ref[used, :, :RANK] = gram


def inverse_kernel(replicas, parts_ref, out_ref):
    terms = jnp.sum(parts_ref[...], axis=0)
    out_ref[:FEWER] = terms[:FEWER]
    for j, column in enumerate(inverse_columns(terms[FEWER] * (1.0 / replicas))):
        out_ref[FEWER + j] = column


def error_kernel(
    replicas, terms_ref, left_ref, grads_ref, errors_ref, out_hbm, right_hbm, q_hbm, out_ref, right_ref, q_ref, sems
):
    rows, cols = grads_ref.shape
    inverse = [terms_ref[SOLVER, FEWER + j] for j in range(RANK)]
    blocks = [terms_ref[SENDER, block] for block in range(rows // LANES - FEWER)]
    blocks += [terms_ref[SOLVER, block] for block in range(FEWER)]
    right = jnp.concatenate(
        [multiplied(inverse, left_ref[:, start : start + LANES]) for start in range(0, cols, LANES)], axis=1
    )
    new_q = jnp.concatenate([multiplied(inverse, block) for block in blocks], axis=1) * (1.0 / replicas)
    right_ref[...] = right * math.sqrt(COLS)
    q_ref[...] = new_q
    copies = [
        pltpu.make_async_copy(right_ref, right_hbm, sems.at[CHUNKS]),
        pltpu.make_async_copy(q_ref, q_hbm, sems.at[CHUNKS + 1]),
    ]
    for copy in copies:
        copy.start()
    q1, q2, q3 = pieces_of(new_q)
    r1, r2, r3 = pieces_of(right)
    tall = stacked(q1, q1, q2, q2, q1, q3)
    wide = stacked(r1, r2, r1, r2, r3, r1)
    step = rows // CHUNKS
    for chunk in range(CHUNKS):
        part = pl.ds(chunk * step, step)
        approx = lax.dot_general(
            tall[:, chunk * step : (chunk + 1) * step],
            wide,
            (((0,), (0,)), ((), ())),
            preferred_element_type=jnp.float32,
        )
        merged = grads_ref[part, :].astype(jnp.float32) + errors_ref[part, :].astype(jnp.float32)
        out_ref[part, :] = (merged - approx).astype(jnp.bfloat16)
        copy = pltpu.make_async_copy(out_ref.at[part, :], out_hbm.at[0, part, :], sems.at[chunk])
        copy.start()
        copies.append(copy)
    for copy in copies:
        copy.wait()


def exchange(value, axes):
    peers = math.prod(lax.axis_size(axis) for axis in axes)
    copies = jnp.broadcast_to(value[None], (peers,) + value.shape)
    return lax.all_to_all(copies, axes, 0, 0, tiled=True)


def on_device(grads, errors, q_in):
    replicas = lax.axis_size("z") * lax.axis_size("x")
    _, rows, cols = grads.shape
    f32, bf16 = jnp.float32, jnp.bfloat16
    left_rows, back_blocks = RANK * cols // LANES, rows // LANES
    limit = pltpu.CompilerParams(vmem_limit_bytes=32 * 2**20)
    q_in, core = lax.optimization_barrier((q_in, lax.axis_index("core")))

    left, grads_near, errors_near = pl.pallas_call(
        left_kernel,
        out_shape=(
            pltpu.VMEM((left_rows, LANES), f32),
            pltpu.VMEM((rows, cols), bf16),
            pltpu.VMEM((rows, cols), bf16),
        ),
        in_specs=[HBM] * 3,
        out_specs=(VMEM, VMEM, VMEM),
        scratch_shapes=[pltpu.VMEM((RANK, rows), f32), pltpu.SemaphoreType.DMA, pltpu.SemaphoreType.DMA((LOADS, 2))],
        compiler_params=limit,
        name="left",
    )(*(pltpu.with_memory_space_constraint(x, pltpu.HBM) for x in (q_in.T, grads, errors)))

    left = jnp.sum(exchange(left, ("x",)), axis=0)
    left, terms = pl.pallas_call(
        functools.partial(back_kernel, replicas),
        out_shape=(
            pltpu.VMEM((RANK, cols), f32),
            pltpu.VMEM((back_blocks + 1, RANK, LANES), f32),
        ),
        in_specs=[VMEM] * 3,
        out_specs=(VMEM, VMEM),
        compiler_params=limit,
        name="back",
    )(exchange(left, ("z",)), grads_near, errors_near)

    terms = jnp.sum(lax.all_gather(terms, "core"), axis=0)

    near, far = ("x", "y_low"), ("z", "y_high")

    def most(terms):
        back = jnp.sum(exchange(terms[: back_blocks - FEWER], near), axis=0)
        return jnp.sum(exchange(back, far), axis=0)

    def rest_and_inverse(terms):
        terms = jnp.sum(exchange(terms[back_blocks - FEWER :], far), axis=0)
        return pl.pallas_call(
            functools.partial(inverse_kernel, replicas),
            out_shape=pltpu.VMEM((FEWER + RANK, RANK, LANES), f32),
            in_specs=[VMEM],
            out_specs=VMEM,
            compiler_params=limit,
            name="inverse",
        )(exchange(terms, near))

    terms, core = lax.optimization_barrier((terms, core))
    terms = lax.cond(core == SENDER, most, rest_and_inverse, terms)
    terms = lax.all_gather(terms, "core")

    new_error, right_factor, new_q = pl.pallas_call(
        functools.partial(error_kernel, replicas),
        out_shape=(
            jax.ShapeDtypeStruct((1, rows, cols), bf16),
            jax.ShapeDtypeStruct((RANK, cols), f32),
            jax.ShapeDtypeStruct((RANK, rows), f32),
        ),
        in_specs=[VMEM] * 4,
        out_specs=(HBM, HBM, HBM),
        scratch_shapes=[
            pltpu.VMEM((rows, cols), bf16),
            pltpu.VMEM((RANK, cols), f32),
            pltpu.VMEM((RANK, rows), f32),
            pltpu.SemaphoreType.DMA((CHUNKS + 2,)),
        ],
        compiler_params=limit,
        name="error",
    )(terms, left, grads_near, errors_near)
    return new_error, right_factor.T, new_q.T


def solution(mesh):
    physical = Mesh(mesh.devices.reshape(8, 8, 4, 2, 2), ("z", "x", "y_high", "y_low", "core"))
    dp, tensor = ("z", "x"), ("y_high", "y_low", "core")
    return jax.shard_map(
        on_device,
        mesh=physical,
        in_specs=(P(dp, None, tensor), P(dp, None, tensor), P()),
        out_specs=(P(dp, None, tensor), P(tensor, None), P()),
        check_vma=False,
    )
```
